512 devices in a mesh: tm: 128 (over z, y, core), rows: 4 (over x).
Axes of the slice: x: 4, y: 8, z: 8, core: 2. Of those that a mesh axis runs over, the one named last changes fastest.
Arguments:
- phases: bfloat16 [256, 512, 512], P('tm', 'rows'), may hold values from -6 to 6
- focal_data: bfloat16 [256, 2, 256, 256], P('tm', None, 'rows'), may hold values from -6 to 6
- shifts: int32 [256, 2], P('tm'), may hold values from 0 to 2, as said below
- pupil_mask: int32 [512, 512], P('rows'), may hold values 0 or 1
Outputs:
- adjoint_field: float32 [256, 512, 512], P('tm', 'rows')
- wind_grad: float32 [2], replicated
The draws below stay inside these ranges and needn't reach their ends.
Inputs may be any that keep to these rules, and one draw needn't show every extreme that they name: `shifts`: column 0 is a frame's shift along pupil rows, 0 or 1, and sums over all frames to exactly 32; column 1 is its shift along pupil columns, 0 to 2.
All inputs are finite; a program needn't handle non-finite values. No bound on the sum of `pupil_mask` on one device may be relied on, other than what follows from the above.
Results may differ from the reference program's by a relative error of at most 0.0054.
Values may be sent and summed in bfloat16 or wider, within the bound.
A program may use at most 128 MiB of HBM per device.

```python
import math
import jax
import jax.numpy as jnp
from jax import lax

PUPIL = 512
FOCAL = 256
FRAMES = 256
ROW_SHIFT_SUM = 32


def draw_shifts(key, part):
    rank_key, side_key = jax.random.split(jax.random.fold_in(key, 11))
    ranking = jax.random.permutation(rank_key, FRAMES)
    down_steps = (ranking < ROW_SHIFT_SUM).astype(jnp.int32)
    side_steps = jax.random.randint(side_key, (FRAMES,), 0, 3, dtype=jnp.int32)
    return jnp.stack([down_steps, side_steps], axis=1)


def touch_ends(result, own_key, smallest, high):
    longest = result.shape.index(max(result.shape))
    spots = []
    for shift in (0, 1):
        where = [jax.random.randint(jax.random.fold_in(own_key, axis), (), 0, length) for axis, length in enumerate(result.shape)]
        where[longest] = (where[longest] + shift) % result.shape[longest]
        spots.append(tuple(where))
    return result.at[spots[0]].set(smallest).at[spots[1]].set(high)


def levels(own_key, extent, cuts, least, top_value):
    level, own = 1.0, jax.random.fold_in(own_key, 6)
    for axis_at, blocks in cuts:
        draws = jnp.exp(jax.random.uniform(jax.random.fold_in(own, axis_at), (blocks,), jnp.float32, least / len(cuts), top_value / len(cuts)))
        level = level * jnp.repeat(draws, extent[axis_at] // blocks).reshape([-1 if axis == axis_at else 1 for axis in range(len(extent))])
    return level


def scatter_about(key, shape, scale, most, shards=(), kind=jnp.bfloat16):
    values = jax.random.normal(key, shape, jnp.float32) * scale
    if len(shards) > 0:
        values = levels(key, shape, shards, -0.22, 0.18) * values
    return jnp.clip(values, min=-most, max=most).astype(kind)


def setup_inputs(seed: int = 0) -> dict:
    streams_of = jax.random.split(jax.random.key(seed), 5)
    phases = scatter_about(streams_of[0], (FRAMES, PUPIL, PUPIL), 1.0, 6.0, ((0, 128), (1, 4)))
    focal_data = scatter_about(streams_of[1], (FRAMES, 2, FOCAL, FOCAL), 1.0, 6.0, ((0, 128), (2, 4)))
    shifts = draw_shifts(jax.random.fold_in(streams_of[4], 71), 0)
    pupil_mask = touch_ends((jax.random.randint(streams_of[3], (PUPIL, PUPIL), 0, 10) < 9).astype(jnp.int32), jax.random.fold_in(streams_of[3], 1), 0, 1)
    return {"phases": phases, "focal_data": focal_data, "shifts": shifts, "pupil_mask": pupil_mask}


decay_rate = 0.999

def tables(first_row, row_total):
    focal_pos = jnp.arange(FOCAL, dtype=jnp.int32) - FOCAL // 2
    pupil_pos = first_row + jnp.arange(row_total, dtype=jnp.int32) - PUPIL // 2
    turns = jnp.mod(focal_pos[:, None] * pupil_pos[None, :], 2 * PUPIL)
    angle = turns.astype(jnp.float32) * (math.pi / PUPIL)
    factor = 1.0 / math.sqrt(PUPIL)
    return ((jnp.cos(angle) * factor).astype(jnp.bfloat16), (-jnp.sin(angle) * factor).astype(jnp.bfloat16))

def shift_back(field_in, shift_rows, shift_cols, pad_rows):
    cols_total = field_in.shape[1]
    padded = jnp.pad(field_in, ((0, pad_rows), (0, 0)))
    start_row = jnp.minimum(shift_rows, pad_rows).astype(jnp.int32)
    moved = lax.dynamic_slice(padded, (start_row, jnp.zeros((), jnp.int32)), field_in.shape)
    start_col = jnp.minimum(shift_cols, cols_total).astype(jnp.int32)
    rolled = jnp.roll(moved, -start_col, axis=1)
    keep = jnp.arange(cols_total, dtype=jnp.int32) < cols_total - start_col
    return jnp.where(keep[None, :], rolled, jnp.zeros_like(rolled))

def frame_gradient(phase_now, live, frame_data, cos_t, sin_t):
    masked = jnp.where(live, phase_now, jnp.zeros_like(phase_now))
    y_real = jnp.dot(masked, cos_t.T, preferred_element_type=jnp.float32).astype(jnp.bfloat16)
    y_imag = jnp.dot(masked, sin_t.T, preferred_element_type=jnp.float32).astype(jnp.bfloat16)
    e_real = jnp.dot(cos_t, y_real, preferred_element_type=jnp.float32) - jnp.dot(sin_t, y_imag, preferred_element_type=jnp.float32)
    e_imag = jnp.dot(cos_t, y_imag, preferred_element_type=jnp.float32) + jnp.dot(sin_t, y_real, preferred_element_type=jnp.float32)
    r_real = (frame_data[0].astype(jnp.float32) - e_real).astype(jnp.bfloat16)
    r_imag = (frame_data[1].astype(jnp.float32) - e_imag).astype(jnp.bfloat16)
    w_real = (jnp.dot(cos_t.T, r_real, preferred_element_type=jnp.float32) + jnp.dot(sin_t.T, r_imag, preferred_element_type=jnp.float32)).astype(jnp.bfloat16)
    w_imag = (jnp.dot(cos_t.T, r_imag, preferred_element_type=jnp.float32) - jnp.dot(sin_t.T, r_real, preferred_element_type=jnp.float32)).astype(jnp.bfloat16)
    summed = jnp.dot(w_real, cos_t, preferred_element_type=jnp.float32) + jnp.dot(w_imag, sin_t, preferred_element_type=jnp.float32)
    return jnp.where(live, summed, jnp.zeros_like(summed))

def reference(phases, focal_data, shifts, pupil_mask):
    cos_t, sin_t = tables(0, PUPIL)
    live = pupil_mask == 1

    def backward(carried, inputs):
        lam_next, wind_sum = carried
        phase_now, frame_data, shift_now = inputs
        grad = frame_gradient(phase_now, live, frame_data, cos_t, sin_t)
        prior = decay_rate * shift_back(lam_next, shift_now[0], shift_now[1], PUPIL)
        lam_now = grad + prior
        phase_wide = phase_now.astype(jnp.float32)
        down_diff = jnp.concatenate([phase_wide[1:], jnp.zeros((1, PUPIL), jnp.float32)], axis=0) - phase_wide
        side_diff = jnp.concatenate([phase_wide[:, 1:], jnp.zeros((PUPIL, 1), jnp.float32)], axis=1) - phase_wide
        wind_sum = wind_sum + jnp.stack([jnp.sum(prior * down_diff), jnp.sum(prior * side_diff)])
        return ((lam_now, wind_sum), lam_now)
    start = (jnp.zeros((PUPIL, PUPIL), jnp.float32), jnp.zeros((2,), jnp.float32))
    (last_lam, wind_sum), adjoint_field = lax.scan(backward, start, (phases, focal_data, shifts), reverse=True)
    return (adjoint_field, -wind_sum / (PUPIL * FRAMES))
```

```python
import functools
import math

import jax
import jax.numpy as jnp
import numpy as np
from jax import lax
from jax.experimental import pallas as pl
from jax.experimental.pallas import tpu as pltpu
from jax.sharding import PartitionSpec as P

PUPIL = 512
FOCAL = 256
HALO = 32
LANES = 128
DECAY = 0.999
MESH = pl.DeviceIdType.MESH
F32 = jnp.float32
BF16 = jnp.bfloat16


def transform_tables():
    focal_pos = np.arange(FOCAL, dtype=np.int32) - FOCAL // 2
    pupil_pos = np.arange(PUPIL, dtype=np.int32) - PUPIL // 2
    turns = np.mod(focal_pos[:, None] * pupil_pos[None, :], 2 * PUPIL)
    angle = turns.astype(np.float32) * np.float32(math.pi / PUPIL)
    factor = np.float32(1.0 / math.sqrt(PUPIL))
    cos_t = (np.cos(angle) * factor).astype(BF16)
    sin_t = (-np.sin(angle) * factor).astype(BF16)
    half = FOCAL // 2
    by_focal = np.concatenate([cos_t[:half], sin_t[:half], cos_t[half:], sin_t[half:]], axis=0)
    return np.ascontiguousarray(by_focal.T), by_focal


def body(
    Y, Z, X, phases, focal, shifts, mask, by_pupil, by_focal, out, wind,
    y_send, y_recv, f_recv, h_send, h_recv, s_recv, t_recv, resid, w_buf, w_recv,
    grad, gb, bseg, cx, ag, ys, zs, ret, cr, carry, ws, wc, wx, wy, wz,
    y_sem, f_sem, h_sem, s_sem, t_sem, w_sem, c_sem, ys_sem, zs_sem, r_sem, cr_sem,
    wc_sem, wx_sem, wy_sem, wz_sem,
):
    BLOCK = PUPIL // X
    WINDOW = BLOCK + HALO
    PIECES = 2 * Y
    PR = WINDOW * 4 // PIECES
    me = lax.axis_index("tm")
    x = lax.axis_index("rows")
    core = lax.rem(me, 2)
    y = lax.rem(me // 2, Y)
    z = me // (2 * Y)
    other = 1 - core

    def at(x_=None, y_=None, z_=None, c_=None):
        zz = z if z_ is None else z_
        yy = y if y_ is None else y_
        cc = core if c_ is None else c_
        return ((zz * Y + yy) * 2 + cc, x if x_ is None else x_)

    def copy(src, dst, sems, n, device):
        return pltpu.make_async_remote_copy(
            src_ref=src, dst_ref=dst, send_sem=sems.at[0, n], recv_sem=sems.at[1, n],
            device_id=device, device_id_type=MESH,
        )

    def start(copies):
        for c in copies:
            c.start()
        return copies

    def arrive(copies):
        for c in copies:
            c.wait_recv()

    waiting = []

    xs = [lax.rem(x + p, X) for p in range(1, X)]
    yy = [lax.rem(y + p, Y) for p in range(1, Y)]
    zz = [lax.rem(z + p, Z) for p in range(1, Z)]

    barrier = pltpu.get_barrier_semaphore()
    for k in xs:
        pl.semaphore_signal(barrier, inc=1, device_id=at(x_=k), device_id_type=MESH)
    for p in range(1, 2 * Y):
        dev = at(y_=lax.rem(y + p // 2, Y), c_=lax.rem(core + p, 2))
        pl.semaphore_signal(barrier, inc=1, device_id=dev, device_id_type=MESH)
    for k in zz:
        pl.semaphore_signal(barrier, inc=1, device_id=at(z_=k), device_id_type=MESH)

    a0, b0, a1, b1 = shifts[0, 0], shifts[0, 1], shifts[1, 0], shifts[1, 1]
    live = jnp.where(mask[...] == 1, 1.0, 0.0).astype(F32)
    h_send[0:HALO] = live[0:HALO].astype(BF16)
    h_send[HALO : HALO + 16] = phases[0, 0:16]
    h_send[HALO + 16 : HALO + 32] = phases[1, 0:16]
    my_line = y * 2 + core
    s_recv[my_line, 0:8] = jnp.full((8, LANES), a0 + a1, jnp.int32)
    s_recv[my_line, 8:16] = jnp.full((8, LANES), b0 + b1, jnp.int32)
    for f in range(2):
        masked = (phases[f].astype(F32) * live).astype(BF16)
        yv = jnp.dot(masked, by_pupil[...], preferred_element_type=F32).astype(BF16)
        y_send[2 * f] = yv[:, 0:256]
        y_send[2 * f + 1] = yv[:, 256:512]

    pl.semaphore_wait(barrier, (X - 1) + (2 * Y - 1) + (Z - 1))

    rows_of = lambda k: pl.ds(pl.multiple_of(k * BLOCK, BLOCK), BLOCK)
    q_rows = FOCAL // X
    q_of = lambda k: pl.ds(pl.multiple_of(k * q_rows, q_rows), q_rows)
    cols_of = lambda k: pl.ds(pl.multiple_of(lax.rem(k, 2) * LANES, LANES), LANES)

    y_copies = start([
        copy(y_send.at[k], y_recv.at[rows_of(x)], y_sem, n, at(x_=k)) for n, k in enumerate(xs)
    ])
    f_copies = start([
        copy(focal.at[k // 2, :, :, cols_of(k)], f_recv.at[:, q_of(x), :], f_sem, n, at(x_=k))
        for n, k in enumerate(xs)
    ])
    s_copies = start([
        copy(s_recv.at[my_line], s_recv.at[my_line], s_sem, p - 1,
             at(y_=lax.rem(y + p // 2, Y), c_=lax.rem(core + p, 2)))
        for p in range(1, 2 * Y)
    ])
    h_copies = start([copy(h_send, h_recv, h_sem, 0, at(x_=lax.rem(x + X - 1, X)))])
    waiting += y_copies + f_copies + s_copies + h_copies

    y_recv[rows_of(x)] = y_send[x]
    f_recv[:, q_of(x), :] = focal[x // 2, :, :, cols_of(x)]
    w_buf[PUPIL : PUPIL + HALO] = jnp.zeros((HALO, 256), BF16)

    arrive(y_copies)
    m = jnp.dot(by_focal[...], y_recv[...], preferred_element_type=F32)
    arrive(f_copies)
    for h in range(2):
        mc, ms = m[256 * h : 256 * h + 128], m[256 * h + 128 : 256 * h + 256]
        e_real = mc[:, 0:128] - ms[:, 128:256]
        e_imag = mc[:, 128:256] + ms[:, 0:128]
        r_real = (f_recv[0, 128 * h : 128 * h + 128].astype(F32) - e_real).astype(BF16)
        r_imag = (f_recv[1, 128 * h : 128 * h + 128].astype(F32) - e_imag).astype(BF16)
        resid[256 * h : 256 * h + 128, 0:128] = r_real
        resid[256 * h : 256 * h + 128, 128:256] = r_imag
        resid[256 * h + 128 : 256 * h + 256, 0:128] = r_imag
        resid[256 * h + 128 : 256 * h + 256, 128:256] = -r_real
    w_buf[0:PUPIL] = jnp.dot(by_pupil[...], resid[...], preferred_element_type=F32).astype(BF16)
    win_of = lambda k: pl.ds(pl.multiple_of(k * BLOCK, BLOCK), WINDOW)
    w_copies = start([
        copy(w_buf.at[win_of(k)], w_recv.at[x], w_sem, n, at(x_=k)) for n, k in enumerate(xs)
    ])
    waiting += w_copies
    w_recv[x] = w_buf[win_of(x)]

    arrive(s_copies)
    total_shift = s_recv[0]
    for l in range(1, 2 * Y):
        total_shift = total_shift + s_recv[l]
    t_recv[z] = total_shift
    t_copies = start([
        copy(t_recv.at[z], t_recv.at[z], t_sem, n, at(z_=k)) for n, k in enumerate(zz)
    ])
    waiting += t_copies
    arrive(t_copies)
    zero_tile = jnp.zeros((16, LANES), jnp.int32)
    beyond = zero_tile
    z_cols = [None] * Z + [zero_tile[8:9]]
    for k in reversed(range(Z)):
        beyond = beyond + jnp.where(k > z, t_recv[k], zero_tile)
        z_cols[k] = z_cols[k + 1] + t_recv[k, 8:9]
    chip_end = beyond[8:9]
    y_cols = [None] * Y + [chip_end]
    own_sum, c0_sum, c1_sum, c2_sum = beyond, beyond, beyond, beyond
    for k in reversed(range(Y)):
        y_cols[k] = y_cols[k + 1] + s_recv[2 * k + 1, 8:9] + s_recv[2 * k, 8:9]
        for c in range(2):
            line = 2 * k + c
            tile = s_recv[line]
            own_sum = own_sum + jnp.where(line >= my_line, tile, zero_tile)
            c0_sum = c0_sum + jnp.where(line >= 2 * y, tile, zero_tile)
            c1_sum = c1_sum + jnp.where(line >= 2 * y + 1, tile, zero_tile)
            c2_sum = c2_sum + jnp.where(line >= 2 * y + 2, tile, zero_tile)
    row0 = jnp.max(own_sum[0:8])
    row1 = row0 - a0
    col0 = jnp.max(own_sum[8:16])
    col1 = col0 - b0
    col2 = col1 - b1
    chip_col0, chip_col1, chip_col2 = c0_sum[8:9], c1_sum[8:9], c2_sum[8:9]

    lane = lax.broadcasted_iota(jnp.int32, (1, LANES), 1)
    wide = lax.broadcasted_iota(jnp.int32, (1, PUPIL), 1)

    def keep(cols, late, early):
        return jnp.where(((cols - late) & (PUPIL - 1)) >= early - late, 1.0, 0.0).astype(F32)

    def block_cols(piece):
        return lax.rem(piece, 4) * LANES + lane

    arrive(h_copies)
    arrive(w_copies)
    for f in range(2):
        g = jnp.dot(w_recv[2 * f], by_focal[0:256], preferred_element_type=F32) + jnp.dot(
            w_recv[2 * f + 1], by_focal[256:512], preferred_element_type=F32
        )
        grad[f, 0:BLOCK] = g[0:BLOCK] * live
        grad[f, BLOCK:WINDOW] = g[BLOCK:WINDOW] * h_recv[0:HALO].astype(F32)
        turned = pltpu.roll(grad[f], (row0, row1)[f], 0)
        gb[f] = pltpu.roll(turned, (col0, col1)[f] & (PUPIL - 1), 1)
    seg = gb[0] + gb[1] * (DECAY * keep(wide, col1, col0))

    def rows_cols(piece):
        r, c = piece // 4, piece % 4
        return slice(PR * r, PR * r + PR), slice(LANES * c, LANES * c + LANES)

    for m_ in range(PIECES):
        r, c = rows_cols(m_)
        bseg[m_ % 2, m_ // 2] = seg[r, c]

    c_copies = start([
        copy(bseg.at[other], cx.at[other], c_sem, 0, at(c_=other)),
        copy(bseg.at[core], cx.at[core], c_sem, 1, at(c_=other)),
    ])
    waiting += c_copies
    arrive(c_copies[0:1])
    first = core == 0
    for k in range(Y):
        mine, theirs = bseg[core, k], cx[core, k]
        early = jnp.where(first, mine, theirs)
        late = jnp.where(first, theirs, mine)
        ag[k] = early + late * (DECAY**2 * keep(block_cols(2 * k + core), chip_col1, chip_col0))
    ys_copies = start([
        copy(ag.at[k], ys.at[y], ys_sem, n, at(y_=k)) for n, k in enumerate(yy)
    ])
    waiting += ys_copies
    ys[y] = ag[y]
    arrive(ys_copies)
    my_cols = block_cols(my_line)
    later = [None] * Y
    later[Y - 1] = jnp.zeros((PR, LANES), F32)
    for k in reversed(range(Y - 1)):
        later[k] = ys[k + 1] + later[k + 1] * (DECAY**4 * keep(my_cols, y_cols[k + 2], y_cols[k + 1]))
    zs[z] = ys[0] + later[0] * (DECAY**4 * keep(my_cols, y_cols[1], y_cols[0]))
    zs_copies = start([
        copy(zs.at[z], zs.at[z], zs_sem, n, at(z_=k)) for n, k in enumerate(zz)
    ])
    waiting += zs_copies
    arrive(zs_copies)
    acc = jnp.zeros((PR, LANES), F32)
    for k in reversed(range(1, Z)):
        new = zs[k] + acc * (DECAY ** (4 * Y) * keep(my_cols, z_cols[k + 1], z_cols[k]))
        acc = jnp.where(k > z, new, acc)
    for k in range(Y):
        ret[k] = later[k] + acc * (
            DECAY ** (4 * (Y - 1 - k)) * keep(my_cols, chip_end, y_cols[k + 1])
        )
    r_copies = start([
        copy(ret.at[k], cr.at[core, y], r_sem, n, at(y_=k)) for n, k in enumerate(yy)
    ])
    waiting += r_copies
    cr[core, y] = ret[y]
    arrive(r_copies)
    cr_copies = start([copy(cr.at[core], cr.at[core], cr_sem, 0, at(c_=other))])
    waiting += cr_copies
    arrive(c_copies[1:2])
    arrive(cr_copies)
    for m_ in range(PIECES):
        r, c = rows_cols(m_)
        chip = cr[m_ % 2, m_ // 2]
        within = cx[m_ % 2, m_ // 2] + chip * (
            DECAY**2 * keep(block_cols(m_), chip_col2, chip_col1)
        )
        carry[r, c] = jnp.where(first, within, chip)

    tiles = [jnp.zeros((8, LANES), F32), jnp.zeros((8, LANES), F32)]
    inner = jnp.where(x < X - 1, 1.0, 0.0).astype(F32)
    prior_b = carry[...] * (DECAY * keep(wide, col2, col1))
    for f in (1, 0):
        moved = pltpu.roll(prior_b, lax.rem(WINDOW - (row0, row1)[f], WINDOW), 0)[0:BLOCK]
        prior = pltpu.roll(moved, (PUPIL - (col0, col1)[f]) & (PUPIL - 1), 1)
        out[f] = grad[f, 0:BLOCK] + prior
        now = phases[f].astype(F32)
        below = h_recv[HALO + 16 * f : HALO + 16 * f + 16].astype(F32)[0:1] * inner
        down = jnp.concatenate([now[1:], below], axis=0) - now
        side = jnp.where(wide == PUPIL - 1, 0.0, pltpu.roll(now, PUPIL - 1, 1)) - now
        for n, diff in enumerate((down, side)):
            prod = jnp.sum((prior * diff).reshape(BLOCK // 8, 8, PUPIL), axis=0)
            for c in range(4):
                tiles[n] = tiles[n] + prod[:, LANES * c : LANES * c + LANES]
        if f == 1:
            prior_b = (gb[1] + prior_b) * (DECAY * keep(wide, col1, col0))

    def add_up(buf, mine, count, sems, devices):
        value = ws[...]
        buf[mine] = value
        copies = start([
            copy(buf.at[mine], buf.at[mine], sems, n, d) for n, d in enumerate(devices)
        ])
        arrive(copies)
        total = buf[0]
        for k in range(1, count):
            total = total + buf[k]
        ws[...] = total
        return copies

    ws[0:8] = tiles[0]
    ws[8:16] = tiles[1]
    waiting += add_up(wc, core, 2, wc_sem, [at(c_=other)])
    waiting += add_up(wx, x, X, wx_sem, [at(x_=k) for k in xs])
    waiting += add_up(wy, y, Y, wy_sem, [at(y_=k) for k in yy])
    waiting += add_up(wz, z, Z, wz_sem, [at(z_=k) for k in zz])
    scale = -1.0 / (PUPIL * 2.0 * 2 * Y * Z)
    wind[0] = jnp.sum(ws[0:8]) * scale
    wind[1] = jnp.sum(ws[8:16]) * scale
    for c in waiting:
        c.wait_send()


def on_device(Y, Z, X, phases, focal, shifts, mask):
    BLOCK = PUPIL // X
    WINDOW = BLOCK + HALO
    PIECES = 2 * Y
    PR = WINDOW * 4 // PIECES
    by_pupil, by_focal = transform_tables()
    vmem = pl.BlockSpec(memory_space=pltpu.VMEM)
    smem = pl.BlockSpec(memory_space=pltpu.SMEM)
    V = pltpu.VMEM

    def sems(n):
        return pltpu.SemaphoreType.DMA((2, n))

    scratch = [
        V((4, BLOCK, 256), BF16),
        V((PUPIL, 256), BF16),
        V((2, FOCAL, LANES), BF16),
        V((HALO + 32, PUPIL), BF16),
        V((HALO + 32, PUPIL), BF16),
        V((2 * Y, 16, LANES), jnp.int32),
        V((Z, 16, LANES), jnp.int32),
        V((PUPIL, 256), BF16),
        V((PUPIL + HALO, 256), BF16),
        V((X, WINDOW, 256), BF16),
        V((2, WINDOW, PUPIL), F32),
        V((2, WINDOW, PUPIL), F32),
        V((2, Y, PR, LANES), F32),
        V((2, Y, PR, LANES), F32),
        V((Y, PR, LANES), F32),
        V((Y, PR, LANES), F32),
        V((Z, PR, LANES), F32),
        V((Y, PR, LANES), F32),
        V((2, Y, PR, LANES), F32),
        V((WINDOW, PUPIL), F32),
        V((16, LANES), F32),
        V((2, 16, LANES), F32),
        V((X, 16, LANES), F32),
        V((Y, 16, LANES), F32),
        V((Z, 16, LANES), F32),
        sems(X), sems(X), sems(1), sems(2 * Y), sems(Z), sems(X), sems(2), sems(Y), sems(Z), sems(Y),
        sems(1), sems(1), sems(X), sems(Y), sems(Z),
    ]
    return pl.pallas_call(
        functools.partial(body, Y, Z, X),
        name="adjoint_sweep",
        out_shape=(
            jax.ShapeDtypeStruct((2, BLOCK, PUPIL), F32),
            jax.ShapeDtypeStruct((2,), F32),
        ),
        in_specs=[vmem, vmem, smem, vmem, vmem, vmem],
        out_specs=(vmem, smem),
        scratch_shapes=scratch,
        compiler_params=pltpu.CompilerParams(
            collective_id=1, has_side_effects=True, vmem_limit_bytes=40 << 20
        ),
    )(phases, focal, shifts, mask, jnp.asarray(by_pupil), jnp.asarray(by_focal))


def solution(mesh):
    X = mesh.shape["rows"]
    count = mesh.shape["tm"]
    Y = 8 if count == 128 else 2
    Z = count // (2 * Y)
    in_specs = (P("tm", "rows", None), P("tm", None, "rows", None), P("tm", None), P("rows", None))
    out_specs = (P("tm", "rows", None), P())
    return jax.shard_map(
        functools.partial(on_device, Y, Z, X), mesh=mesh, in_specs=in_specs, out_specs=out_specs,
        check_vma=False,
    )
```

```python
import functools
import math

import jax
import jax.numpy as jnp
import numpy as np
from jax import lax
from jax.experimental import pallas as pl
from jax.experimental.pallas import tpu as pltpu
from jax.sharding import PartitionSpec as P

PUPIL = 512
FOCAL = 256
HALO = 32
LANES = 128
DECAY = 0.999
MESH = pl.DeviceIdType.MESH
F32 = jnp.float32
BF16 = jnp.bfloat16


def transform_tables():
    focal_pos = np.arange(FOCAL, dtype=np.int32) - FOCAL // 2
    pupil_pos = np.arange(PUPIL, dtype=np.int32) - PUPIL // 2
    turns = np.mod(focal_pos[:, None] * pupil_pos[None, :], 2 * PUPIL)
    angle = turns.astype(np.float32) * np.float32(math.pi / PUPIL)
    factor = np.float32(1.0 / math.sqrt(PUPIL))
    cos_t = (np.cos(angle) * factor).astype(BF16)
    sin_t = (-np.sin(angle) * factor).astype(BF16)
    half = FOCAL // 2
    by_focal = np.concatenate([cos_t[:half], sin_t[:half], cos_t[half:], sin_t[half:]], axis=0)
    return np.ascontiguousarray(by_focal.T), by_focal


def body(
    Y, Z, X, phases_h, focal_h, shifts_h, mask_h, by_pupil_h, by_focal_h, out_h, wind,
    phases, shifts, mask, by_pupil, by_focal,
    y_send, y_recv, f_recv, h_send, h_recv, s_recv, t_recv, resid, w_buf, w_recv,
    grad, gb, bseg, cx, ag, ys, zs, ret, cr, carry, diffs, d0b, qseg, qx, qc, qy, wz, wy, wx, out,
    in_sem, out_sem, y_sem, f_sem, h_sem, s_sem, t_sem, w_sem, c_sem, ys_sem, zs_sem, r_sem, cr_sem,
    qx_sem, qy_sem, wz_sem, wy_sem, wx_sem,
):
    BLOCK = PUPIL // X
    WINDOW = BLOCK + HALO
    PIECES = 2 * Y
    PR = WINDOW * 4 // PIECES
    PR16 = -(-PR // 16) * 16
    me = lax.axis_index("tm")
    x = lax.axis_index("rows")
    core = lax.rem(me, 2)
    y = lax.rem(me // 2, Y)
    z = me // (2 * Y)
    other = 1 - core

    def at(x_=None, y_=None, z_=None, c_=None):
        zz = z if z_ is None else z_
        yy = y if y_ is None else y_
        cc = core if c_ is None else c_
        return ((zz * Y + yy) * 2 + cc, x if x_ is None else x_)

    def copy(src, dst, sems, n, device):
        return pltpu.make_async_remote_copy(
            src_ref=src, dst_ref=dst, send_sem=sems.at[0, n], recv_sem=sems.at[1, n],
            device_id=device, device_id_type=MESH,
        )

    def start(copies):
        for c in copies:
            c.start()
        return copies

    def arrive(copies):
        for c in copies:
            c.wait_recv()

    waiting = []

    xs = [lax.rem(x + p, X) for p in range(1, X)]
    yy = [lax.rem(y + p, Y) for p in range(1, Y)]
    zz = [lax.rem(z + p, Z) for p in range(1, Z)]

    zs[...] = jnp.zeros((Z, PR, LANES), F32)
    barrier = pltpu.get_barrier_semaphore()
    for k in xs:
        pl.semaphore_signal(barrier, inc=1, device_id=at(x_=k), device_id_type=MESH)
    for p in range(1, 2 * Y):
        dev = at(y_=lax.rem(y + p // 2, Y), c_=lax.rem(core + p, 2))
        pl.semaphore_signal(barrier, inc=1, device_id=dev, device_id_type=MESH)
    for k in zz:
        pl.semaphore_signal(barrier, inc=1, device_id=at(z_=k), device_id_type=MESH)

    q_rows = FOCAL // X
    q_of = lambda k: pl.ds(pl.multiple_of(k * q_rows, q_rows), q_rows)
    cols_of = lambda k: pl.ds(pl.multiple_of(lax.rem(k, 2) * LANES, LANES), LANES)
    loads = [
        pltpu.make_async_copy(src, dst, in_sem.at[n])
        for n, (src, dst) in enumerate([
            (shifts_h, shifts),
            (phases_h, phases),
            (mask_h, mask),
            (by_pupil_h, by_pupil),
            (by_focal_h, by_focal),
            (focal_h.at[x // 2, :, :, cols_of(x)], f_recv.at[:, q_of(x), :]),
        ])
    ]
    for load in loads:
        load.start()

    for load in loads[0:3]:
        load.wait()
    a0, b0, a1, b1 = shifts[0, 0], shifts[0, 1], shifts[1, 0], shifts[1, 1]
    live = jnp.where(mask[...] == 1, 1.0, 0.0).astype(F32)
    h_send[0:HALO] = live[0:HALO].astype(BF16)
    h_send[HALO : HALO + 16] = phases[0, 0:16]
    h_send[HALO + 16 : HALO + 32] = phases[1, 0:16]
    my_line = y * 2 + core
    s_recv[my_line, 0:8] = jnp.full((8, LANES), a0 + a1, jnp.int32)
    s_recv[my_line, 8:16] = jnp.full((8, LANES), b0 + b1, jnp.int32)
    loads[3].wait()
    for f in range(2):
        masked = (phases[f].astype(F32) * live).astype(BF16)
        yv = jnp.dot(masked, by_pupil[...], preferred_element_type=F32).astype(BF16)
        y_send[2 * f] = yv[:, 0:256]
        y_send[2 * f + 1] = yv[:, 256:512]

    pl.semaphore_wait(barrier, (X - 1) + (2 * Y - 1) + (Z - 1))

    rows_of = lambda k: pl.ds(pl.multiple_of(k * BLOCK, BLOCK), BLOCK)
    y_copies = start([
        copy(y_send.at[k], y_recv.at[rows_of(x)], y_sem, n, at(x_=k)) for n, k in enumerate(xs)
    ])
    s_copies = start([
        copy(s_recv.at[my_line], s_recv.at[my_line], s_sem, p - 1,
             at(y_=lax.rem(y + p // 2, Y), c_=lax.rem(core + p, 2)))
        for p in range(1, 2 * Y)
    ])
    f_copies = start([
        copy(focal_h.at[k // 2, :, :, cols_of(k)], f_recv.at[:, q_of(x), :], f_sem, n, at(x_=k))
        for n, k in enumerate(xs)
    ])
    h_copies = start([copy(h_send, h_recv, h_sem, 0, at(x_=lax.rem(x + X - 1, X)))])
    waiting += y_copies + f_copies + s_copies + h_copies

    y_recv[rows_of(x)] = y_send[x]
    w_buf[PUPIL : PUPIL + HALO] = jnp.zeros((HALO, 256), BF16)
    if PR16 > PR:
        ret[:, PR:PR16] = jnp.zeros((Y, PR16 - PR, LANES), BF16)

    arrive(y_copies)
    loads[4].wait()
    m = jnp.dot(by_focal[...], y_recv[...], preferred_element_type=F32)
    arrive(s_copies)
    total_shift = s_recv[0]
    for l in range(1, 2 * Y):
        total_shift = total_shift + s_recv[l]
    t_recv[z] = total_shift
    t_copies = start([
        copy(t_recv.at[z], t_recv.at[z], t_sem, n, at(z_=k)) for n, k in enumerate(zz)
    ])
    waiting += t_copies
    loads[5].wait()
    arrive(f_copies)
    for h in range(2):
        mc, ms = m[256 * h : 256 * h + 128], m[256 * h + 128 : 256 * h + 256]
        e_real = mc[:, 0:128] - ms[:, 128:256]
        e_imag = mc[:, 128:256] + ms[:, 0:128]
        r_real = (f_recv[0, 128 * h : 128 * h + 128].astype(F32) - e_real).astype(BF16)
        r_imag = (f_recv[1, 128 * h : 128 * h + 128].astype(F32) - e_imag).astype(BF16)
        resid[256 * h : 256 * h + 128, 0:128] = r_real
        resid[256 * h : 256 * h + 128, 128:256] = r_imag
        resid[256 * h + 128 : 256 * h + 256, 0:128] = r_imag
        resid[256 * h + 128 : 256 * h + 256, 128:256] = -r_real
    w_buf[0:PUPIL] = jnp.dot(by_pupil[...], resid[...], preferred_element_type=F32).astype(BF16)
    win_of = lambda k: pl.ds(pl.multiple_of(k * BLOCK, BLOCK), WINDOW)
    w_copies = start([
        copy(w_buf.at[win_of(k)], w_recv.at[x], w_sem, n, at(x_=k)) for n, k in enumerate(xs)
    ])
    waiting += w_copies
    w_recv[x] = w_buf[win_of(x)]

    lane = lax.broadcasted_iota(jnp.int32, (1, LANES), 1)
    wide = lax.broadcasted_iota(jnp.int32, (1, PUPIL), 1)

    arrive(h_copies)
    inner = jnp.where(x < X - 1, 1.0, 0.0).astype(F32)
    for f in range(2):
        now = phases[f].astype(F32)
        below = h_recv[HALO + 16 * f : HALO + 16 * f + 16].astype(F32)[0:1] * inner
        diffs[f, 0, 0:BLOCK] = jnp.concatenate([now[1:], below], axis=0) - now
        diffs[f, 1, 0:BLOCK] = jnp.where(wide == PUPIL - 1, 0.0, pltpu.roll(now, PUPIL - 1, 1)) - now
        for n in range(2):
            diffs[f, n, BLOCK:WINDOW] = jnp.zeros((HALO, PUPIL), F32)
    arrive(t_copies)
    zero_tile = jnp.zeros((16, LANES), jnp.int32)
    beyond = zero_tile
    z_cols = [None] * Z + [zero_tile[8:9]]
    for k in reversed(range(Z)):
        beyond = beyond + jnp.where(k > z, t_recv[k], zero_tile)
        z_cols[k] = z_cols[k + 1] + t_recv[k, 8:9]
    chip_end = beyond[8:9]
    y_cols = [None] * Y + [chip_end]
    own_sum, c0_sum, c1_sum, c2_sum = beyond, beyond, beyond, beyond
    for k in reversed(range(Y)):
        y_cols[k] = y_cols[k + 1] + s_recv[2 * k + 1, 8:9] + s_recv[2 * k, 8:9]
        for c in range(2):
            line = 2 * k + c
            tile = s_recv[line]
            own_sum = own_sum + jnp.where(line >= my_line, tile, zero_tile)
            c0_sum = c0_sum + jnp.where(line >= 2 * y, tile, zero_tile)
            c1_sum = c1_sum + jnp.where(line >= 2 * y + 1, tile, zero_tile)
            c2_sum = c2_sum + jnp.where(line >= 2 * y + 2, tile, zero_tile)
    row0 = jnp.max(own_sum[0:8])
    row1 = row0 - a0
    col0 = jnp.max(own_sum[8:16])
    col1 = col0 - b0
    col2 = col1 - b1
    chip_col0, chip_col1, chip_col2 = c0_sum[8:9], c1_sum[8:9], c2_sum[8:9]

    def keep(cols, late, early):
        return jnp.where(((cols - late) & (PUPIL - 1)) >= early - late, 1.0, 0.0).astype(F32)

    def block_cols(piece):
        return lax.rem(piece, 4) * LANES + lane

    def rows_cols(piece):
        r, c = piece // 4, piece % 4
        return slice(PR * r, PR * r + PR), slice(LANES * c, LANES * c + LANES)

    def shifted(value, f):
        turned = pltpu.roll(value, (row0, row1)[f], 0)
        return pltpu.roll(turned, (col0, col1)[f] & (PUPIL - 1), 1)

    def folded(value):
        parts = jnp.sum(value.reshape(value.shape[0] // 8, 8, value.shape[1]), axis=0)
        total = parts[:, 0:LANES]
        for c in range(1, value.shape[1] // LANES):
            total = total + parts[:, LANES * c : LANES * c + LANES]
        return total

    keep_01 = DECAY * keep(wide, col1, col0)
    keep_12 = DECAY * keep(wide, col2, col1)
    for n in range(2):
        d0b[n] = keep_01 * shifted(diffs[0, n], 0)
        weight = keep_12 * (shifted(diffs[1, n], 1) + d0b[n])
        for m_ in range(PIECES):
            r, c = rows_cols(m_)
            qseg[m_ % 2, m_ // 2, n] = weight[r, c]
    qx_copies = start([copy(qseg.at[other], qx, qx_sem, 0, at(c_=other))])
    waiting += qx_copies

    arrive(w_copies)
    for f in range(2):
        g = jnp.dot(w_recv[2 * f], by_focal[0:256], preferred_element_type=F32) + jnp.dot(
            w_recv[2 * f + 1], by_focal[256:512], preferred_element_type=F32
        )
        grad[f, 0:BLOCK] = g[0:BLOCK] * live
        grad[f, BLOCK:WINDOW] = g[BLOCK:WINDOW] * h_recv[0:HALO].astype(F32)
        gb[f] = shifted(grad[f], f)
    seg = gb[0] + gb[1] * keep_01

    for m_ in range(PIECES):
        r, c = rows_cols(m_)
        bseg[m_ % 2, m_ // 2] = seg[r, c]

    c_copies = start([
        copy(bseg.at[other], cx.at[other], c_sem, 0, at(c_=other)),
        copy(bseg.at[core], cx.at[core], c_sem, 1, at(c_=other)),
    ])
    waiting += c_copies
    arrive(c_copies[0:1])
    first = core == 0
    for k in range(Y):
        mine, theirs = bseg[core, k], cx[core, k]
        early = jnp.where(first, mine, theirs)
        late = jnp.where(first, theirs, mine)
        ag[k] = early + late * (DECAY**2 * keep(block_cols(2 * k + core), chip_col1, chip_col0))
    ys_copies = start([
        copy(ag.at[k], ys.at[y], ys_sem, n, at(y_=k)) for n, k in enumerate(yy)
    ])
    waiting += ys_copies
    ys[y] = ag[y]
    arrive(qx_copies)
    tiles = [folded(gb[1] * d0b[n]) for n in range(2)]
    for k in range(Y):
        late = jnp.where(first, cx[core, k], bseg[core, k])
        keep_k = DECAY**2 * keep(block_cols(2 * k + core), chip_col2, chip_col1)
        for n in range(2):
            mine, theirs = qseg[core, k, n], qx[k, n]
            early_q = jnp.where(first, mine, theirs)
            late_q = jnp.where(first, theirs, mine)
            tiles[n] = tiles[n] + folded(late * early_q)
            qc[k, n] = late_q + keep_k * early_q
    qy_copies = start([
        copy(qc.at[k], qy.at[y], qy_sem, n, at(y_=k)) for n, k in enumerate(yy)
    ])
    waiting += qy_copies
    qy[y] = qc[y]
    arrive(ys_copies)
    my_cols = block_cols(my_line)
    later = [None] * Y
    later[Y - 1] = jnp.zeros((PR, LANES), F32)
    for k in reversed(range(Y - 1)):
        later[k] = ys[k + 1] + later[k + 1] * (DECAY**4 * keep(my_cols, y_cols[k + 2], y_cols[k + 1]))
    zs[z] = ys[0] + later[0] * (DECAY**4 * keep(my_cols, y_cols[1], y_cols[0]))
    zs_copies = [copy(zs.at[z], zs.at[z], zs_sem, n, at(z_=k)) for n, k in enumerate(zz)]
    for n, k in enumerate(zz):
        pl.when(k < z)(zs_copies[n].start)
    reach = [
        DECAY ** (4 * (Y - 1 - k)) * keep(my_cols, chip_end, y_cols[k + 1]) for k in range(Y)
    ]
    arrive(qy_copies)
    whole = [jnp.zeros((PR, LANES), F32) for _ in range(2)]
    for k in range(Y):
        for n in range(2):
            tiles[n] = tiles[n] + folded(later[k] * qy[k, n])
            whole[n] = whole[n] + reach[k] * qy[k, n]
    for n in range(len(zz)):
        pl.when(lax.rem(z + Z - 1 - n, Z) > z)(zs_copies[n].wait_recv)
    acc = jnp.zeros((PR, LANES), F32)
    for k in reversed(range(1, Z)):
        new = zs[k] + acc * (DECAY ** (4 * Y) * keep(my_cols, z_cols[k + 1], z_cols[k]))
        acc = jnp.where(k > z, new, acc)
    for k in range(Y):
        ret[k, 0:PR] = (later[k] + acc * reach[k]).astype(BF16)
    r_copies = start([
        copy(ret.at[k], cr.at[core, y], r_sem, n, at(y_=k)) for n, k in enumerate(yy)
    ])
    waiting += r_copies
    cr[core, y] = ret[y]

    def send_sums(buf, mine, sems, devices):
        copies = start([
            copy(buf.at[mine], buf.at[mine], sems, n, d) for n, d in enumerate(devices)
        ])
        waiting.extend(copies)
        return copies

    def summed(buf, count):
        total = buf[0]
        for k in range(1, count):
            total = total + buf[k]
        return total

    for n in range(2):
        wz[z, 8 * n : 8 * n + 8] = tiles[n] + folded(acc * whole[n])
    wz_copies = send_sums(wz, z, wz_sem, [at(z_=k) for k in zz])
    arrive(wz_copies)
    wy[my_line] = summed(wz, Z)
    wy_copies = send_sums(
        wy, my_line, wy_sem,
        [at(y_=lax.rem(y + p // 2, Y), c_=lax.rem(core + p, 2)) for p in range(1, 2 * Y)],
    )
    arrive(r_copies)
    cr_copies = start([copy(cr.at[core], cr.at[core], cr_sem, 0, at(c_=other))])
    waiting += cr_copies
    arrive(c_copies[1:2])
    arrive(cr_copies)
    for m_ in range(PIECES):
        r, c = rows_cols(m_)
        chip = cr[m_ % 2, m_ // 2].astype(F32)[0:PR]
        within = cx[m_ % 2, m_ // 2] + chip * (
            DECAY**2 * keep(block_cols(m_), chip_col2, chip_col1)
        )
        carry[r, c] = jnp.where(first, within, chip)

    prior_b = carry[...] * keep_12
    stores = []
    for f in (1, 0):
        moved = pltpu.roll(prior_b, lax.rem(WINDOW - (row0, row1)[f], WINDOW), 0)[0:BLOCK]
        prior = pltpu.roll(moved, (PUPIL - (col0, col1)[f]) & (PUPIL - 1), 1)
        out[f] = grad[f, 0:BLOCK] + prior
        stores.append(pltpu.make_async_copy(out.at[f], out_h.at[f], out_sem.at[f]))
        stores[-1].start()
        if f == 1:
            prior_b = (gb[1] + prior_b) * keep_01

    arrive(wy_copies)
    wx[x] = summed(wy, 2 * Y)
    wx_copies = send_sums(wx, x, wx_sem, [at(x_=k) for k in xs])
    arrive(wx_copies)
    total = summed(wx, X)
    scale = -1.0 / (PUPIL * 2.0 * 2 * Y * Z)
    wind[0] = jnp.sum(total[0:8]) * scale
    wind[1] = jnp.sum(total[8:16]) * scale
    for n, k in enumerate(zz):
        pl.when(k < z)(zs_copies[n].wait_send)
    for store in stores:
        store.wait()
    for c in waiting:
        c.wait_send()


def on_device(Y, Z, X, phases, focal, shifts, mask):
    BLOCK = PUPIL // X
    WINDOW = BLOCK + HALO
    PIECES = 2 * Y
    PR = WINDOW * 4 // PIECES
    PR16 = -(-PR // 16) * 16
    by_pupil, by_focal = transform_tables()
    smem = pl.BlockSpec(memory_space=pltpu.SMEM)
    hbm = pl.BlockSpec(memory_space=pltpu.HBM)
    V = pltpu.VMEM

    def sems(n):
        return pltpu.SemaphoreType.DMA((2, n))

    scratch = [
        V((2, BLOCK, PUPIL), BF16),
        pltpu.SMEM((2, 2), jnp.int32),
        V((BLOCK, PUPIL), jnp.int32),
        V((PUPIL, PUPIL), BF16),
        V((PUPIL, PUPIL), BF16),
        V((4, BLOCK, 256), BF16),
        V((PUPIL, 256), BF16),
        V((2, FOCAL, LANES), BF16),
        V((HALO + 32, PUPIL), BF16),
        V((HALO + 32, PUPIL), BF16),
        V((2 * Y, 16, LANES), jnp.int32),
        V((Z, 16, LANES), jnp.int32),
        V((PUPIL, 256), BF16),
        V((PUPIL + HALO, 256), BF16),
        V((X, WINDOW, 256), BF16),
        V((2, WINDOW, PUPIL), F32),
        V((2, WINDOW, PUPIL), F32),
        V((2, Y, PR, LANES), F32),
        V((2, Y, PR, LANES), F32),
        V((Y, PR, LANES), F32),
        V((Y, PR, LANES), F32),
        V((Z, PR, LANES), F32),
        V((Y, PR16, LANES), BF16),
        V((2, Y, PR16, LANES), BF16),
        V((WINDOW, PUPIL), F32),
        V((2, 2, WINDOW, PUPIL), F32),
        V((2, WINDOW, PUPIL), F32),
        V((2, Y, 2, PR, LANES), F32),
        V((Y, 2, PR, LANES), F32),
        V((Y, 2, PR, LANES), F32),
        V((Y, 2, PR, LANES), F32),
        V((Z, 16, LANES), F32),
        V((2 * Y, 16, LANES), F32),
        V((X, 16, LANES), F32),
        V((2, BLOCK, PUPIL), F32),
        pltpu.SemaphoreType.DMA((6,)),
        pltpu.SemaphoreType.DMA((2,)),
        sems(X), sems(X), sems(1), sems(2 * Y), sems(Z), sems(X), sems(2), sems(Y), sems(Z), sems(Y),
        sems(1), sems(1), sems(Y), sems(Z), sems(2 * Y), sems(X),
    ]
    return pl.pallas_call(
        functools.partial(body, Y, Z, X),
        name="adjoint_sweep",
        out_shape=(
            jax.ShapeDtypeStruct((2, BLOCK, PUPIL), F32),
            jax.ShapeDtypeStruct((2,), F32),
        ),
        in_specs=[hbm] * 6,
        out_specs=(hbm, smem),
        scratch_shapes=scratch,
        compiler_params=pltpu.CompilerParams(
            collective_id=1, has_side_effects=True, vmem_limit_bytes=63 << 20
        ),
    )(phases, focal, shifts, mask, jnp.asarray(by_pupil), jnp.asarray(by_focal))


def solution(mesh):
    X = mesh.shape["rows"]
    count = mesh.shape["tm"]
    Y = 8 if count == 128 else 2
    Z = count // (2 * Y)
    in_specs = (P("tm", "rows", None), P("tm", None, "rows", None), P("tm", None), P("rows", None))
    out_specs = (P("tm", "rows", None), P())
    return jax.shard_map(
        functools.partial(on_device, Y, Z, X), mesh=mesh, in_specs=in_specs, out_specs=out_specs,
        check_vma=False,
    )
```

```python
import functools
import math

import jax
import jax.numpy as jnp
import numpy as np
from jax import lax
from jax.experimental import pallas as pl
from jax.experimental.pallas import tpu as pltpu
from jax.sharding import PartitionSpec as P

PUPIL = 512
FOCAL = 256
HALO = 32
LANES = 128
DECAY = 0.999
MESH = pl.DeviceIdType.MESH
F32 = jnp.float32
BF16 = jnp.bfloat16


def transform_tables():
    focal_pos = np.arange(FOCAL, dtype=np.int32) - FOCAL // 2
    pupil_pos = np.arange(PUPIL, dtype=np.int32) - PUPIL // 2
    turns = np.mod(focal_pos[:, None] * pupil_pos[None, :], 2 * PUPIL)
    angle = turns.astype(np.float32) * np.float32(math.pi / PUPIL)
    factor = np.float32(1.0 / math.sqrt(PUPIL))
    cos_t = (np.cos(angle) * factor).astype(BF16)
    sin_t = (-np.sin(angle) * factor).astype(BF16)
    half = FOCAL // 2
    by_focal = np.concatenate([cos_t[:half], sin_t[:half], cos_t[half:], sin_t[half:]], axis=0)
    return np.ascontiguousarray(by_focal.T), by_focal


def body(
    Y, Z, X, phases_h, focal_h, shifts_h, mask_h, by_pupil_h, by_focal_h, out_h, wind,
    phases, shifts, mask, by_pupil, by_focal,
    y_send, y_recv, f_recv, h_send, h_recv, s_recv, t_recv, resid, w_buf, w_recv,
    grad, gb, bseg, cx, ag, ys, zs, ret, cr, carry, diffs, d0b, qseg, qx, qc, qy, wz, wy, wx, out,
    in_sem, out_sem, y_sem, f_sem, h_sem, s_sem, t_sem, w_sem, c_sem, ys_sem, zs_sem, r_sem, cr_sem,
    qx_sem, qy_sem, wz_sem, wy_sem, wx_sem,
):
    BLOCK = PUPIL // X
    WINDOW = BLOCK + HALO
    PIECES = 2 * Y
    PR = WINDOW * 4 // PIECES
    PR16 = -(-PR // 16) * 16
    me = lax.axis_index("tm")
    x = lax.axis_index("rows")
    core = lax.rem(me, 2)
    y = lax.rem(me // 2, Y)
    z = me // (2 * Y)
    other = 1 - core

    def at(x_=None, y_=None, z_=None, c_=None):
        zz = z if z_ is None else z_
        yy = y if y_ is None else y_
        cc = core if c_ is None else c_
        return ((zz * Y + yy) * 2 + cc, x if x_ is None else x_)

    def copy(src, dst, sems, n, device):
        return pltpu.make_async_remote_copy(
            src_ref=src, dst_ref=dst, send_sem=sems.at[0, n], recv_sem=sems.at[1, n],
            device_id=device, device_id_type=MESH,
        )

    def start(copies):
        for c in copies:
            c.start()
        return copies

    def arrive(copies):
        for c in copies:
            c.wait_recv()

    waiting = []

    def far_first(n):
        return sorted(range(1, n), key=lambda p: -min(p, n - p))

    xs = [lax.rem(x + p, X) for p in far_first(X)]
    yy = [lax.rem(y + p, Y) for p in far_first(Y)]
    zz = [lax.rem(z + p, Z) for p in far_first(Z)]
    lines = [
        at(y_=lax.rem(y + p, Y), c_=lax.rem(core + q, 2))
        for p in far_first(Y) for q in range(2)
    ] + [at(c_=other)]

    zs[...] = jnp.zeros((Z, PR, LANES), F32)
    barrier = pltpu.get_barrier_semaphore()
    for k in xs:
        pl.semaphore_signal(barrier, inc=1, device_id=at(x_=k), device_id_type=MESH)
    for dev in [at(z_=k) for k in zz] + lines:
        pl.semaphore_signal(barrier, inc=1, device_id=dev, device_id_type=MESH)

    q_rows = FOCAL // X
    q_of = lambda k: pl.ds(pl.multiple_of(k * q_rows, q_rows), q_rows)
    cols_of = lambda k: pl.ds(pl.multiple_of(lax.rem(k, 2) * LANES, LANES), LANES)
    loads = [
        pltpu.make_async_copy(src, dst, in_sem.at[n])
        for n, (src, dst) in enumerate([
            (shifts_h, shifts),
            (phases_h, phases),
            (mask_h, mask),
            (by_pupil_h, by_pupil.at[0:PUPIL]),
            (by_focal_h, by_focal),
            (focal_h.at[x // 2, :, :, cols_of(x)], f_recv.at[:, q_of(x), :]),
        ])
    ]
    for load in loads:
        load.start()

    for load in loads[0:3]:
        load.wait()
    a0, b0, a1, b1 = shifts[0, 0], shifts[0, 1], shifts[1, 0], shifts[1, 1]
    live = jnp.where(mask[...] == 1, 1.0, 0.0).astype(F32)
    h_send[0:HALO] = live[0:HALO].astype(BF16)
    h_send[HALO : HALO + 16] = phases[0, 0:16]
    h_send[HALO + 16 : HALO + 32] = phases[1, 0:16]
    my_line = y * 2 + core
    s_recv[my_line, 0:1] = jnp.full((1, LANES), a0 + a1, jnp.int32)
    s_recv[my_line, 1:2] = jnp.full((1, LANES), b0 + b1, jnp.int32)
    loads[3].wait()
    for f in range(2):
        masked = (phases[f].astype(F32) * live).astype(BF16)
        yv = jnp.dot(masked, by_pupil[0:PUPIL], preferred_element_type=F32).astype(BF16)
        y_send[2 * f] = yv[:, 0:256]
        y_send[2 * f + 1] = yv[:, 256:512]

    pl.semaphore_wait(barrier, (X - 1) + (2 * Y - 1) + (Z - 1))

    rows_of = lambda k: pl.ds(pl.multiple_of(k * BLOCK, BLOCK), BLOCK)
    y_copies = start([
        copy(y_send.at[k], y_recv.at[rows_of(x)], y_sem, n, at(x_=k)) for n, k in enumerate(xs)
    ])
    s_copies = start([
        copy(s_recv.at[my_line], s_recv.at[my_line], s_sem, n, dev) for n, dev in enumerate(lines)
    ])
    f_copies = start([
        copy(focal_h.at[k // 2, :, :, cols_of(k)], f_recv.at[:, q_of(x), :], f_sem, n, at(x_=k))
        for n, k in enumerate(xs)
    ])
    h_copies = start([copy(h_send, h_recv, h_sem, 0, at(x_=lax.rem(x + X - 1, X)))])
    waiting += y_copies + f_copies + s_copies + h_copies

    y_recv[rows_of(x)] = y_send[x]
    by_pupil[PUPIL : PUPIL + HALO] = jnp.zeros((HALO, PUPIL), BF16)
    if PR16 > PR:
        ret[:, PR:PR16] = jnp.zeros((Y, PR16 - PR, LANES), BF16)

    arrive(y_copies)
    loads[4].wait()
    m = jnp.dot(by_focal[...], y_recv[...], preferred_element_type=F32)
    arrive(s_copies)
    total_shift = s_recv[0]
    for l in range(1, 2 * Y):
        total_shift = total_shift + s_recv[l]
    t_recv[z] = total_shift
    t_copies = start([
        copy(t_recv.at[z], t_recv.at[z], t_sem, n, at(z_=k)) for n, k in enumerate(zz)
    ])
    waiting += t_copies
    loads[5].wait()
    arrive(f_copies)
    for h in range(2):
        mc, ms = m[256 * h : 256 * h + 128], m[256 * h + 128 : 256 * h + 256]
        e_real = mc[:, 0:128] - ms[:, 128:256]
        e_imag = mc[:, 128:256] + ms[:, 0:128]
        r_real = (f_recv[0, 128 * h : 128 * h + 128].astype(F32) - e_real).astype(BF16)
        r_imag = (f_recv[1, 128 * h : 128 * h + 128].astype(F32) - e_imag).astype(BF16)
        resid[256 * h : 256 * h + 128, 0:128] = r_real
        resid[256 * h : 256 * h + 128, 128:256] = r_imag
        resid[256 * h + 128 : 256 * h + 256, 0:128] = r_imag
        resid[256 * h + 128 : 256 * h + 256, 128:256] = -r_real
    win_of = lambda k: pl.ds(pl.multiple_of(k * BLOCK, BLOCK), WINDOW)
    w_copies = []
    for n, k in enumerate(xs + [x]):
        rows = jnp.dot(by_pupil[win_of(k)], resid[...], preferred_element_type=F32)
        if n == X - 1:
            w_recv[x] = rows.astype(BF16)
        else:
            w_buf[n] = rows.astype(BF16)
            w_copies += start([copy(w_buf.at[n], w_recv.at[x], w_sem, n, at(x_=k))])
    waiting += w_copies

    lane = lax.broadcasted_iota(jnp.int32, (1, LANES), 1)
    wide = lax.broadcasted_iota(jnp.int32, (1, PUPIL), 1)

    arrive(h_copies)
    inner = jnp.where(x < X - 1, 1.0, 0.0).astype(F32)
    for f in range(2):
        now = phases[f].astype(F32)
        below = h_recv[HALO + 16 * f : HALO + 16 * f + 16].astype(F32)[0:1] * inner
        diffs[f, 0, 0:BLOCK] = jnp.concatenate([now[1:], below], axis=0) - now
        diffs[f, 1, 0:BLOCK] = jnp.where(wide == PUPIL - 1, 0.0, pltpu.roll(now, PUPIL - 1, 1)) - now
        for n in range(2):
            diffs[f, n, BLOCK:WINDOW] = jnp.zeros((HALO, PUPIL), F32)
    arrive(t_copies)
    zero_tile = jnp.zeros((2, LANES), jnp.int32)
    beyond = zero_tile
    z_cols = [None] * Z + [zero_tile[1:2]]
    for k in reversed(range(Z)):
        beyond = beyond + jnp.where(k > z, t_recv[k], zero_tile)
        z_cols[k] = z_cols[k + 1] + t_recv[k, 1:2]
    chip_end = beyond[1:2]
    y_cols = [None] * Y + [chip_end]
    own_sum, c0_sum, c1_sum, c2_sum = beyond, beyond, beyond, beyond
    for k in reversed(range(Y)):
        y_cols[k] = y_cols[k + 1] + s_recv[2 * k + 1, 1:2] + s_recv[2 * k, 1:2]
        for c in range(2):
            line = 2 * k + c
            tile = s_recv[line]
            own_sum = own_sum + jnp.where(line >= my_line, tile, zero_tile)
            c0_sum = c0_sum + jnp.where(line >= 2 * y, tile, zero_tile)
            c1_sum = c1_sum + jnp.where(line >= 2 * y + 1, tile, zero_tile)
            c2_sum = c2_sum + jnp.where(line >= 2 * y + 2, tile, zero_tile)
    row0 = jnp.max(own_sum[0:1])
    row1 = row0 - a0
    col0 = jnp.max(own_sum[1:2])
    col1 = col0 - b0
    col2 = col1 - b1
    chip_col0, chip_col1, chip_col2 = c0_sum[1:2], c1_sum[1:2], c2_sum[1:2]

    def keep(cols, late, early):
        return jnp.where(((cols - late) & (PUPIL - 1)) >= early - late, 1.0, 0.0).astype(F32)

    def block_cols(piece):
        return lax.rem(piece, 4) * LANES + lane

    def rows_cols(piece):
        r, c = piece // 4, piece % 4
        return slice(PR * r, PR * r + PR), slice(LANES * c, LANES * c + LANES)

    def shifted(value, f):
        turned = pltpu.roll(value, (row0, row1)[f], 0)
        return pltpu.roll(turned, (col0, col1)[f] & (PUPIL - 1), 1)

    def folded(value):
        parts = jnp.sum(value.reshape(value.shape[0] // 8, 8, value.shape[1]), axis=0)
        total = parts[:, 0:LANES]
        for c in range(1, value.shape[1] // LANES):
            total = total + parts[:, LANES * c : LANES * c + LANES]
        return total

    keep_01 = DECAY * keep(wide, col1, col0)
    keep_12 = DECAY * keep(wide, col2, col1)
    for n in range(2):
        d0b[n] = keep_01 * shifted(diffs[0, n], 0)
        weight = keep_12 * (shifted(diffs[1, n], 1) + d0b[n])
        for m_ in range(PIECES):
            r, c = rows_cols(m_)
            qseg[m_ % 2, m_ // 2, n] = weight[r, c]
    qx_copies = start([copy(qseg.at[other], qx, qx_sem, 0, at(c_=other))])
    waiting += qx_copies

    arrive(w_copies)
    for f in range(2):
        g = jnp.dot(w_recv[2 * f], by_focal[0:256], preferred_element_type=F32) + jnp.dot(
            w_recv[2 * f + 1], by_focal[256:512], preferred_element_type=F32
        )
        grad[f, 0:BLOCK] = g[0:BLOCK] * live
        grad[f, BLOCK:WINDOW] = g[BLOCK:WINDOW] * h_recv[0:HALO].astype(F32)
        gb[f] = shifted(grad[f], f)
    seg = gb[0] + gb[1] * keep_01

    for m_ in range(PIECES):
        r, c = rows_cols(m_)
        bseg[m_ % 2, m_ // 2] = seg[r, c]

    c_copies = start([
        copy(bseg.at[other], cx.at[other], c_sem, 0, at(c_=other)),
        copy(bseg.at[core], cx.at[core], c_sem, 1, at(c_=other)),
    ])
    waiting += c_copies
    arrive(c_copies[0:1])
    first = core == 0
    for k in range(Y):
        mine, theirs = bseg[core, k], cx[core, k]
        early = jnp.where(first, mine, theirs)
        late = jnp.where(first, theirs, mine)
        ag[k] = early + late * (DECAY**2 * keep(block_cols(2 * k + core), chip_col1, chip_col0))
    ys_copies = start([
        copy(ag.at[k], ys.at[y], ys_sem, n, at(y_=k)) for n, k in enumerate(yy)
    ])
    waiting += ys_copies
    ys[y] = ag[y]
    arrive(qx_copies)
    tiles = [folded(gb[1] * d0b[n]) for n in range(2)]
    for k in range(Y):
        late = jnp.where(first, cx[core, k], bseg[core, k])
        keep_k = DECAY**2 * keep(block_cols(2 * k + core), chip_col2, chip_col1)
        for n in range(2):
            mine, theirs = qseg[core, k, n], qx[k, n]
            early_q = jnp.where(first, mine, theirs)
            late_q = jnp.where(first, theirs, mine)
            tiles[n] = tiles[n] + folded(late * early_q)
            qc[k, n] = late_q + keep_k * early_q
    qy_copies = start([
        copy(qc.at[k], qy.at[y], qy_sem, n, at(y_=k)) for n, k in enumerate(yy)
    ])
    waiting += qy_copies
    qy[y] = qc[y]
    arrive(ys_copies)
    my_cols = block_cols(my_line)
    later = [None] * Y
    later[Y - 1] = jnp.zeros((PR, LANES), F32)
    for k in reversed(range(Y - 1)):
        later[k] = ys[k + 1] + later[k + 1] * (DECAY**4 * keep(my_cols, y_cols[k + 2], y_cols[k + 1]))
    zs[z] = ys[0] + later[0] * (DECAY**4 * keep(my_cols, y_cols[1], y_cols[0]))
    zs_copies = [copy(zs.at[z], zs.at[z], zs_sem, n, at(z_=k)) for n, k in enumerate(zz)]
    for n, k in enumerate(zz):
        pl.when(k < z)(zs_copies[n].start)
    reach = [
        DECAY ** (4 * (Y - 1 - k)) * keep(my_cols, chip_end, y_cols[k + 1]) for k in range(Y)
    ]
    arrive(qy_copies)
    whole = [jnp.zeros((PR, LANES), F32) for _ in range(2)]
    for k in range(Y):
        for n in range(2):
            tiles[n] = tiles[n] + folded(later[k] * qy[k, n])
            whole[n] = whole[n] + reach[k] * qy[k, n]
    for n, p in enumerate(far_first(Z)):
        pl.when(lax.rem(z + Z - p, Z) > z)(zs_copies[n].wait_recv)
    acc = jnp.zeros((PR, LANES), F32)
    for k in reversed(range(1, Z)):
        new = zs[k] + acc * (DECAY ** (4 * Y) * keep(my_cols, z_cols[k + 1], z_cols[k]))
        acc = jnp.where(k > z, new, acc)
    for k in range(Y):
        ret[k, 0:PR] = (later[k] + acc * reach[k]).astype(BF16)
    r_copies = start([
        copy(ret.at[k], cr.at[core, y], r_sem, n, at(y_=k)) for n, k in enumerate(yy)
    ])
    waiting += r_copies
    cr[core, y] = ret[y]

    def send_sums(buf, mine, sems, devices):
        copies = start([
            copy(buf.at[mine], buf.at[mine], sems, n, d) for n, d in enumerate(devices)
        ])
        waiting.extend(copies)
        return copies

    def summed(buf, count):
        total = buf[0]
        for k in range(1, count):
            total = total + buf[k]
        return total

    for n in range(2):
        wz[z, n : n + 1] = jnp.sum(tiles[n] + folded(acc * whole[n]), axis=0, keepdims=True)
    wz_copies = send_sums(wz, z, wz_sem, [at(z_=k) for k in zz])
    arrive(wz_copies)
    wy[my_line] = summed(wz, Z)
    wy_copies = send_sums(wy, my_line, wy_sem, lines)
    arrive(r_copies)
    cr_copies = start([copy(cr.at[core], cr.at[core], cr_sem, 0, at(c_=other))])
    waiting += cr_copies
    arrive(c_copies[1:2])
    arrive(cr_copies)
    for m_ in range(PIECES):
        r, c = rows_cols(m_)
        chip = cr[m_ % 2, m_ // 2].astype(F32)[0:PR]
        within = cx[m_ % 2, m_ // 2] + chip * (
            DECAY**2 * keep(block_cols(m_), chip_col2, chip_col1)
        )
        carry[r, c] = jnp.where(first, within, chip)

    prior_b = carry[...] * keep_12
    stores = []
    for f in (1, 0):
        moved = pltpu.roll(prior_b, lax.rem(WINDOW - (row0, row1)[f], WINDOW), 0)[0:BLOCK]
        prior = pltpu.roll(moved, (PUPIL - (col0, col1)[f]) & (PUPIL - 1), 1)
        out[f] = grad[f, 0:BLOCK] + prior
        stores.append(pltpu.make_async_copy(out.at[f], out_h.at[f], out_sem.at[f]))
        stores[-1].start()
        if f == 1:
            prior_b = (gb[1] + prior_b) * keep_01

    arrive(wy_copies)
    wx[x] = summed(wy, 2 * Y)
    wx_copies = send_sums(wx, x, wx_sem, [at(x_=k) for k in xs])
    arrive(wx_copies)
    total = summed(wx, X)
    scale = -1.0 / (PUPIL * 2.0 * 2 * Y * Z)
    wind[0] = jnp.sum(total[0:1]) * scale
    wind[1] = jnp.sum(total[1:2]) * scale
    for n, k in enumerate(zz):
        pl.when(k < z)(zs_copies[n].wait_send)
    for store in stores:
        store.wait()
    for c in waiting:
        c.wait_send()


def finish(field_h, sums_h, out_h, wind_h, sem):
    frames = field_h.shape[0]
    parts = 4
    rows = field_h.shape[1] // parts
    copies = [pltpu.make_async_copy(sums_h, wind_h, sem.at[0])]
    for f in range(frames):
        for p in range(parts):
            here = (f, pl.ds(p * rows, rows))
            copies.append(
                pltpu.make_async_copy(field_h.at[here], out_h.at[here], sem.at[1 + f * parts + p])
            )
    for c in copies:
        c.start()
    for c in copies:
        c.wait()


def on_device(Y, Z, X, phases, focal, shifts, mask):
    BLOCK = PUPIL // X
    WINDOW = BLOCK + HALO
    PIECES = 2 * Y
    PR = WINDOW * 4 // PIECES
    PR16 = -(-PR // 16) * 16
    by_pupil, by_focal = transform_tables()
    smem = pl.BlockSpec(memory_space=pltpu.SMEM)
    hbm = pl.BlockSpec(memory_space=pltpu.HBM)
    V = pltpu.VMEM

    def sems(n):
        return pltpu.SemaphoreType.DMA((2, n))

    scratch = [
        V((2, BLOCK, PUPIL), BF16),
        pltpu.SMEM((2, 2), jnp.int32),
        V((BLOCK, PUPIL), jnp.int32),
        V((PUPIL + HALO, PUPIL), BF16),
        V((PUPIL, PUPIL), BF16),
        V((4, BLOCK, 256), BF16),
        V((PUPIL, 256), BF16),
        V((2, FOCAL, LANES), BF16),
        V((HALO + 32, PUPIL), BF16),
        V((HALO + 32, PUPIL), BF16),
        V((2 * Y, 2, LANES), jnp.int32),
        V((Z, 2, LANES), jnp.int32),
        V((PUPIL, 256), BF16),
        V((X, WINDOW, 256), BF16),
        V((X, WINDOW, 256), BF16),
        V((2, WINDOW, PUPIL), F32),
        V((2, WINDOW, PUPIL), F32),
        V((2, Y, PR, LANES), F32),
        V((2, Y, PR, LANES), F32),
        V((Y, PR, LANES), F32),
        V((Y, PR, LANES), F32),
        V((Z, PR, LANES), F32),
        V((Y, PR16, LANES), BF16),
        V((2, Y, PR16, LANES), BF16),
        V((WINDOW, PUPIL), F32),
        V((2, 2, WINDOW, PUPIL), F32),
        V((2, WINDOW, PUPIL), F32),
        V((2, Y, 2, PR, LANES), F32),
        V((Y, 2, PR, LANES), F32),
        V((Y, 2, PR, LANES), F32),
        V((Y, 2, PR, LANES), F32),
        V((Z, 2, LANES), F32),
        V((2 * Y, 2, LANES), F32),
        V((X, 2, LANES), F32),
        V((2, BLOCK, PUPIL), F32),
        pltpu.SemaphoreType.DMA((6,)),
        pltpu.SemaphoreType.DMA((2,)),
        sems(X), sems(X), sems(1), sems(2 * Y), sems(Z), sems(X), sems(2), sems(Y), sems(Z), sems(Y),
        sems(1), sems(1), sems(Y), sems(Z), sems(2 * Y), sems(X),
    ]
    shapes = (
        jax.ShapeDtypeStruct((2, BLOCK, PUPIL), F32),
        jax.ShapeDtypeStruct((2,), F32),
    )
    field, sums = pl.pallas_call(
        functools.partial(body, Y, Z, X),
        name="adjoint_sweep",
        out_shape=shapes,
        in_specs=[hbm] * 6,
        out_specs=(hbm, smem),
        scratch_shapes=scratch,
        compiler_params=pltpu.CompilerParams(
            collective_id=1, has_side_effects=True, vmem_limit_bytes=63 << 20
        ),
    )(phases, focal, shifts, mask, jnp.asarray(by_pupil), jnp.asarray(by_focal))
    return pl.pallas_call(
        finish,
        name="finish",
        out_shape=shapes,
        in_specs=[hbm, hbm],
        out_specs=(hbm, hbm),
        scratch_shapes=[pltpu.SemaphoreType.DMA((9,))],
        compiler_params=pltpu.CompilerParams(vmem_limit_bytes=63 << 20),
    )(field, sums)


def solution(mesh):
    X = mesh.shape["rows"]
    count = mesh.shape["tm"]
    Y = 8 if count == 128 else 2
    Z = count // (2 * Y)
    in_specs = (P("tm", "rows", None), P("tm", None, "rows", None), P("tm", None), P("rows", None))
    out_specs = (P("tm", "rows", None), P())
    return jax.shard_map(
        functools.partial(on_device, Y, Z, X), mesh=mesh, in_specs=in_specs, out_specs=out_specs,
        check_vma=False,
    )
```

```python
import functools
import math

import jax
import jax.numpy as jnp
import numpy as np
from jax import lax
from jax.experimental import pallas as pl
from jax.experimental.pallas import tpu as pltpu
from jax.sharding import PartitionSpec as P

PUPIL = 512
FOCAL = 256
HALO = 32
LANES = 128
DECAY = 0.999
MESH = pl.DeviceIdType.MESH
F32 = jnp.float32
BF16 = jnp.bfloat16


def transform_tables():
    focal_pos = np.arange(FOCAL, dtype=np.int32) - FOCAL // 2
    pupil_pos = np.arange(PUPIL, dtype=np.int32) - PUPIL // 2
    turns = np.mod(focal_pos[:, None] * pupil_pos[None, :], 2 * PUPIL)
    angle = turns.astype(np.float32) * np.float32(math.pi / PUPIL)
    factor = np.float32(1.0 / math.sqrt(PUPIL))
    cos_t = (np.cos(angle) * factor).astype(BF16)
    sin_t = (-np.sin(angle) * factor).astype(BF16)
    half = FOCAL // 2
    by_focal = np.concatenate([cos_t[:half], sin_t[:half], cos_t[half:], sin_t[half:]], axis=0)
    return np.ascontiguousarray(by_focal.T), by_focal


def body(
    Y, Z, X, phases_h, focal_h, shifts_h, mask_h, by_pupil_h, by_focal_h, out_h, wind,
    phases, shifts, mask, by_pupil, by_focal,
    y_send, y_recv, f_recv, h_send, h_recv, p_send, p_recv, s_recv, t_recv, resid, w_buf, w_recv,
    grad, gb, bseg, cx, ag, ys, zs, ret, cr, carry, diffs, d0b, qseg, qx, qc, qy, wz, wy, out,
    in_sem, out_sem, y_sem, f_sem, h_sem, s_sem, t_sem, w_sem, c_sem, ys_sem, zs_sem, r_sem, cr_sem,
    qx_sem, qy_sem, wz_sem, wy_sem, sc_sem, ring_sem,
):
    BLOCK = PUPIL // X
    WINDOW = BLOCK + HALO
    PIECES = 2 * Y
    PR = WINDOW * 4 // PIECES
    PR16 = -(-PR // 16) * 16
    me = lax.axis_index("tm")
    x = lax.axis_index("rows")
    core = lax.rem(me, 2)
    y = lax.rem(me // 2, Y)
    z = me // (2 * Y)
    other = 1 - core

    def at(x_=None, y_=None, z_=None, c_=None):
        zz = z if z_ is None else z_
        yy = y if y_ is None else y_
        cc = core if c_ is None else c_
        return ((zz * Y + yy) * 2 + cc, x if x_ is None else x_)

    def copy(src, dst, sems, n, device):
        return pltpu.make_async_remote_copy(
            src_ref=src, dst_ref=dst, send_sem=sems.at[0, n], recv_sem=sems.at[1, n],
            device_id=device, device_id_type=MESH,
        )

    def start(copies):
        for c in copies:
            c.start()
        return copies

    def arrive(copies):
        for c in copies:
            c.wait_recv()

    waiting = []

    def far_first(n):
        return sorted(range(1, n), key=lambda p: -min(p, n - p))

    xs = [lax.rem(x + p, X) for p in far_first(X)]
    yy = [lax.rem(y + p, Y) for p in far_first(Y)]
    zz = [lax.rem(z + p, Z) for p in far_first(Z)]
    lines = [
        at(y_=lax.rem(y + p, Y), c_=lax.rem(core + q, 2))
        for p in far_first(Y) for q in range(2)
    ] + [at(c_=other)]

    zs[...] = jnp.zeros((Z, PR, LANES), F32)
    def ring(d):
        near_y = [at(y_=lax.rem(y + p, Y)) for p in sorted({d % Y, -d % Y})]
        return near_y + [at(z_=lax.rem(z + p, Z)) for p in sorted({d % Z, -d % Z})]

    rounds = [d for d in (1, 2) if 2 * d < max(Y, Z)]

    def announce(n):
        for dev in ring(rounds[n]):
            pl.semaphore_signal(ring_sem.at[n], inc=1, device_id=dev, device_id_type=MESH)

    def heard(n):
        pl.semaphore_wait(ring_sem.at[n], len(ring(rounds[n])))

    barrier = pltpu.get_barrier_semaphore()
    entry = [at(x_=k) for k in xs] + ring(1) + [at(c_=other)]
    for dev in entry:
        pl.semaphore_signal(barrier, inc=1, device_id=dev, device_id_type=MESH)
    q_rows = FOCAL // X
    q_of = lambda k: pl.ds(pl.multiple_of(k * q_rows, q_rows), q_rows)
    cols_of = lambda k: pl.ds(pl.multiple_of(lax.rem(k, 2) * LANES, LANES), LANES)
    loads = [
        pltpu.make_async_copy(src, dst, in_sem.at[n])
        for n, (src, dst) in enumerate([
            (shifts_h, shifts),
            (phases_h, phases),
            (mask_h, mask),
            (by_pupil_h, by_pupil.at[0:PUPIL]),
            (by_focal_h, by_focal),
            (focal_h.at[x // 2, :, :, cols_of(x)], f_recv.at[:, q_of(x), :]),
        ])
    ]
    for load in loads:
        load.start()

    for load in loads[0:3]:
        load.wait()
    a0, b0, a1, b1 = shifts[0, 0], shifts[0, 1], shifts[1, 0], shifts[1, 1]
    live = jnp.where(mask[...] == 1, 1.0, 0.0).astype(F32)
    h_send[0:HALO] = live[0:HALO].astype(BF16)
    for f in range(2):
        p_send[f : f + 1] = phases[f, 0:16].astype(F32)[0:1]
    my_line = y * 2 + core
    s_recv[y, core, 0:1] = jnp.full((1, LANES), a0 + a1, jnp.int32)
    s_recv[y, core, 1:2] = jnp.full((1, LANES), b0 + b1, jnp.int32)
    pl.semaphore_wait(barrier, len(entry))
    if rounds:
        announce(0)
    sc_copies = start([copy(s_recv.at[y, core], s_recv.at[y, core], sc_sem, 0, at(c_=other))])
    waiting += sc_copies
    loads[3].wait()
    for f in range(2):
        masked = (phases[f].astype(F32) * live).astype(BF16)
        yv = jnp.dot(masked, by_pupil[0:PUPIL], preferred_element_type=F32).astype(BF16)
        y_send[2 * f] = yv[:, 0:256]
        y_send[2 * f + 1] = yv[:, 256:512]


    rows_of = lambda k: pl.ds(pl.multiple_of(k * BLOCK, BLOCK), BLOCK)
    y_copies = start([
        copy(y_send.at[k], y_recv.at[rows_of(x)], y_sem, n, at(x_=k)) for n, k in enumerate(xs)
    ])
    f_copies = start([
        copy(focal_h.at[k // 2, :, :, cols_of(k)], f_recv.at[:, q_of(x), :], f_sem, n, at(x_=k))
        for n, k in enumerate(xs)
    ])
    above = at(x_=lax.rem(x + X - 1, X))
    h_copies = start([
        copy(p_send, p_recv, h_sem, 0, above), copy(h_send, h_recv, h_sem, 1, above)
    ])
    waiting += y_copies + f_copies + h_copies
    for n in range(len(rounds)):
        heard(n)
        if n + 1 < len(rounds):
            announce(n + 1)
    arrive(sc_copies)
    s_copies = start([
        copy(s_recv.at[y], s_recv.at[y], s_sem, n, at(y_=k)) for n, k in enumerate(yy)
    ])
    waiting += s_copies

    y_recv[rows_of(x)] = y_send[x]
    by_pupil[PUPIL : PUPIL + HALO] = jnp.zeros((HALO, PUPIL), BF16)
    if PR16 > PR:
        ret[:, PR:PR16] = jnp.zeros((Y, PR16 - PR, LANES), BF16)

    arrive(y_copies)
    loads[4].wait()
    m = jnp.dot(by_focal[...], y_recv[...], preferred_element_type=F32)
    loads[5].wait()
    arrive(f_copies)
    for h in range(2):
        mc, ms = m[256 * h : 256 * h + 128], m[256 * h + 128 : 256 * h + 256]
        e_real = mc[:, 0:128] - ms[:, 128:256]
        e_imag = mc[:, 128:256] + ms[:, 0:128]
        r_real = (f_recv[0, 128 * h : 128 * h + 128].astype(F32) - e_real).astype(BF16)
        r_imag = (f_recv[1, 128 * h : 128 * h + 128].astype(F32) - e_imag).astype(BF16)
        resid[256 * h : 256 * h + 128, 0:128] = r_real
        resid[256 * h : 256 * h + 128, 128:256] = r_imag
        resid[256 * h + 128 : 256 * h + 256, 0:128] = r_imag
        resid[256 * h + 128 : 256 * h + 256, 128:256] = -r_real
    win_of = lambda k: pl.ds(pl.multiple_of(k * BLOCK, BLOCK), WINDOW)
    w_copies = []
    for n, k in enumerate(xs + [x]):
        rows = jnp.dot(by_pupil[win_of(k)], resid[...], preferred_element_type=F32)
        if n == X - 1:
            w_recv[x] = rows.astype(BF16)
        else:
            w_buf[n] = rows.astype(BF16)
            w_copies += start([copy(w_buf.at[n], w_recv.at[x], w_sem, n, at(x_=k))])
    waiting += w_copies

    arrive(s_copies)
    total_shift = jnp.zeros((2, LANES), jnp.int32)
    for k in range(Y):
        for c in range(2):
            total_shift = total_shift + s_recv[k, c]
    t_recv[z] = total_shift
    t_copies = start([
        copy(t_recv.at[z], t_recv.at[z], t_sem, n, at(z_=k)) for n, k in enumerate(zz)
    ])
    waiting += t_copies

    lane = lax.broadcasted_iota(jnp.int32, (1, LANES), 1)
    wide = lax.broadcasted_iota(jnp.int32, (1, PUPIL), 1)

    arrive(h_copies)
    inner = jnp.where(x < X - 1, 1.0, 0.0).astype(F32)
    for f in range(2):
        now = phases[f].astype(F32)
        below = p_recv[f : f + 1] * inner
        diffs[f, 0, 0:BLOCK] = jnp.concatenate([now[1:], below], axis=0) - now
        diffs[f, 1, 0:BLOCK] = jnp.where(wide == PUPIL - 1, 0.0, pltpu.roll(now, PUPIL - 1, 1)) - now
        for n in range(2):
            diffs[f, n, BLOCK:WINDOW] = jnp.zeros((HALO, PUPIL), F32)
    arrive(t_copies)
    zero_tile = jnp.zeros((2, LANES), jnp.int32)
    beyond = zero_tile
    z_cols = [None] * Z + [zero_tile[1:2]]
    for k in reversed(range(Z)):
        beyond = beyond + jnp.where(k > z, t_recv[k], zero_tile)
        z_cols[k] = z_cols[k + 1] + t_recv[k, 1:2]
    chip_end = beyond[1:2]
    y_cols = [None] * Y + [chip_end]
    own_sum, c0_sum, c1_sum, c2_sum = beyond, beyond, beyond, beyond
    for k in reversed(range(Y)):
        y_cols[k] = y_cols[k + 1] + s_recv[k, 1, 1:2] + s_recv[k, 0, 1:2]
        for c in range(2):
            line = 2 * k + c
            tile = s_recv[k, c]
            own_sum = own_sum + jnp.where(line >= my_line, tile, zero_tile)
            c0_sum = c0_sum + jnp.where(line >= 2 * y, tile, zero_tile)
            c1_sum = c1_sum + jnp.where(line >= 2 * y + 1, tile, zero_tile)
            c2_sum = c2_sum + jnp.where(line >= 2 * y + 2, tile, zero_tile)
    row0 = jnp.max(own_sum[0:1])
    row1 = row0 - a0
    col0 = jnp.max(own_sum[1:2])
    col1 = col0 - b0
    col2 = col1 - b1
    chip_col0, chip_col1, chip_col2 = c0_sum[1:2], c1_sum[1:2], c2_sum[1:2]

    def keep(cols, late, early):
        return jnp.where(((cols - late) & (PUPIL - 1)) >= early - late, 1.0, 0.0).astype(F32)

    def block_cols(piece):
        return lax.rem(piece, 4) * LANES + lane

    def rows_cols(piece):
        r, c = piece // 4, piece % 4
        return slice(PR * r, PR * r + PR), slice(LANES * c, LANES * c + LANES)

    def shifted(value, f):
        turned = pltpu.roll(value, (row0, row1)[f], 0)
        return pltpu.roll(turned, (col0, col1)[f] & (PUPIL - 1), 1)

    def folded(value):
        parts = jnp.sum(value.reshape(value.shape[0] // 8, 8, value.shape[1]), axis=0)
        total = parts[:, 0:LANES]
        for c in range(1, value.shape[1] // LANES):
            total = total + parts[:, LANES * c : LANES * c + LANES]
        return total

    keep_01 = DECAY * keep(wide, col1, col0)
    keep_12 = DECAY * keep(wide, col2, col1)
    for n in range(2):
        d0b[n] = keep_01 * shifted(diffs[0, n], 0)
        weight = keep_12 * (shifted(diffs[1, n], 1) + d0b[n])
        for m_ in range(PIECES):
            r, c = rows_cols(m_)
            qseg[m_ % 2, m_ // 2, n] = weight[r, c]
    qx_copies = start([copy(qseg.at[other], qx, qx_sem, 0, at(c_=other))])
    waiting += qx_copies

    arrive(w_copies)
    for f in range(2):
        g = jnp.dot(w_recv[2 * f], by_focal[0:256], preferred_element_type=F32) + jnp.dot(
            w_recv[2 * f + 1], by_focal[256:512], preferred_element_type=F32
        )
        grad[f, 0:BLOCK] = g[0:BLOCK] * live
        grad[f, BLOCK:WINDOW] = g[BLOCK:WINDOW] * h_recv[0:HALO].astype(F32)
        gb[f] = shifted(grad[f], f)
    seg = gb[0] + gb[1] * keep_01

    for m_ in range(PIECES):
        r, c = rows_cols(m_)
        bseg[m_ % 2, m_ // 2] = seg[r, c]

    c_copies = start([
        copy(bseg.at[other], cx.at[other], c_sem, 0, at(c_=other)),
        copy(bseg.at[core], cx.at[core], c_sem, 1, at(c_=other)),
    ])
    waiting += c_copies
    arrive(c_copies[0:1])
    first = core == 0
    for k in range(Y):
        mine, theirs = bseg[core, k], cx[core, k]
        early = jnp.where(first, mine, theirs)
        late = jnp.where(first, theirs, mine)
        ag[k] = early + late * (DECAY**2 * keep(block_cols(2 * k + core), chip_col1, chip_col0))
    ys_copies = start([
        copy(ag.at[k], ys.at[y], ys_sem, n, at(y_=k)) for n, k in enumerate(yy)
    ])
    waiting += ys_copies
    ys[y] = ag[y]
    arrive(qx_copies)
    tiles = [folded(gb[1] * d0b[n]) for n in range(2)]
    for k in range(Y):
        late = jnp.where(first, cx[core, k], bseg[core, k])
        keep_k = DECAY**2 * keep(block_cols(2 * k + core), chip_col2, chip_col1)
        for n in range(2):
            mine, theirs = qseg[core, k, n], qx[k, n]
            early_q = jnp.where(first, mine, theirs)
            late_q = jnp.where(first, theirs, mine)
            tiles[n] = tiles[n] + folded(late * early_q)
            qc[k, n] = late_q + keep_k * early_q
    qy_copies = start([
        copy(qc.at[k], qy.at[y], qy_sem, n, at(y_=k)) for n, k in enumerate(yy)
    ])
    waiting += qy_copies
    qy[y] = qc[y]
    arrive(ys_copies)
    my_cols = block_cols(my_line)
    later = [None] * Y
    later[Y - 1] = jnp.zeros((PR, LANES), F32)
    for k in reversed(range(Y - 1)):
        later[k] = ys[k + 1] + later[k + 1] * (DECAY**4 * keep(my_cols, y_cols[k + 2], y_cols[k + 1]))
    zs[z] = ys[0] + later[0] * (DECAY**4 * keep(my_cols, y_cols[1], y_cols[0]))
    zs_copies = [copy(zs.at[z], zs.at[z], zs_sem, n, at(z_=k)) for n, k in enumerate(zz)]
    for n, k in enumerate(zz):
        pl.when(k < z)(zs_copies[n].start)
    reach = [
        DECAY ** (4 * (Y - 1 - k)) * keep(my_cols, chip_end, y_cols[k + 1]) for k in range(Y)
    ]
    arrive(qy_copies)
    whole = [jnp.zeros((PR, LANES), F32) for _ in range(2)]
    for k in range(Y):
        for n in range(2):
            tiles[n] = tiles[n] + folded(later[k] * qy[k, n])
            whole[n] = whole[n] + reach[k] * qy[k, n]
    for n, p in enumerate(far_first(Z)):
        pl.when(lax.rem(z + Z - p, Z) > z)(zs_copies[n].wait_recv)
    acc = jnp.zeros((PR, LANES), F32)
    for k in reversed(range(1, Z)):
        new = zs[k] + acc * (DECAY ** (4 * Y) * keep(my_cols, z_cols[k + 1], z_cols[k]))
        acc = jnp.where(k > z, new, acc)
    for k in range(Y):
        ret[k, 0:PR] = (later[k] + acc * reach[k]).astype(BF16)
    r_copies = start([
        copy(ret.at[k], cr.at[core, y], r_sem, n, at(y_=k)) for n, k in enumerate(yy)
    ])
    waiting += r_copies
    cr[core, y] = ret[y]

    for n in range(2):
        wz[z, x, n : n + 1] = jnp.sum(tiles[n] + folded(acc * whole[n]), axis=0, keepdims=True)
    cross = sorted(
        ((p, q) for p in range(Z) for q in range(X) if p or q),
        key=lambda t: -min(t[0], Z - t[0]) - min(t[1], X - t[1]),
    )
    wz_copies = start([
        copy(wz.at[z, x], wz.at[z, x], wz_sem, n, at(z_=lax.rem(z + p, Z), x_=lax.rem(x + q, X)))
        for n, (p, q) in enumerate(cross)
    ])
    waiting += wz_copies
    arrive(wz_copies)
    sums = jnp.zeros((2, LANES), F32)
    for k in range(Z):
        for q in range(X):
            sums = sums + wz[k, q]
    wy[my_line] = sums
    wy_copies = start([
        copy(wy.at[my_line], wy.at[my_line], wy_sem, n, dev) for n, dev in enumerate(lines)
    ])
    waiting += wy_copies
    arrive(r_copies)
    cr_copies = start([copy(cr.at[core], cr.at[core], cr_sem, 0, at(c_=other))])
    waiting += cr_copies
    arrive(c_copies[1:2])
    arrive(cr_copies)
    for m_ in range(PIECES):
        r, c = rows_cols(m_)
        chip = cr[m_ % 2, m_ // 2].astype(F32)[0:PR]
        within = cx[m_ % 2, m_ // 2] + chip * (
            DECAY**2 * keep(block_cols(m_), chip_col2, chip_col1)
        )
        carry[r, c] = jnp.where(first, within, chip)

    prior_b = carry[...] * keep_12
    stores = []
    for f in (1, 0):
        moved = pltpu.roll(prior_b, lax.rem(WINDOW - (row0, row1)[f], WINDOW), 0)[0:BLOCK]
        prior = pltpu.roll(moved, (PUPIL - (col0, col1)[f]) & (PUPIL - 1), 1)
        out[f] = grad[f, 0:BLOCK] + prior
        stores.append(pltpu.make_async_copy(out.at[f], out_h.at[f], out_sem.at[f]))
        stores[-1].start()
        if f == 1:
            prior_b = (gb[1] + prior_b) * keep_01

    arrive(wy_copies)
    total = wy[0]
    for k in range(1, 2 * Y):
        total = total + wy[k]
    scale = -1.0 / (PUPIL * 2.0 * 2 * Y * Z)
    wind[0] = jnp.sum(total[0:1]) * scale
    wind[1] = jnp.sum(total[1:2]) * scale
    for n, k in enumerate(zz):
        pl.when(k < z)(zs_copies[n].wait_send)
    for store in stores:
        store.wait()
    for c in waiting:
        c.wait_send()


def on_device(Y, Z, X, phases, focal, shifts, mask):
    BLOCK = PUPIL // X
    WINDOW = BLOCK + HALO
    PIECES = 2 * Y
    PR = WINDOW * 4 // PIECES
    PR16 = -(-PR // 16) * 16
    by_pupil, by_focal = transform_tables()
    smem = pl.BlockSpec(memory_space=pltpu.SMEM)
    hbm = pl.BlockSpec(memory_space=pltpu.HBM)
    V = pltpu.VMEM

    def sems(n):
        return pltpu.SemaphoreType.DMA((2, n))

    scratch = [
        V((2, BLOCK, PUPIL), BF16),
        pltpu.SMEM((2, 2), jnp.int32),
        V((BLOCK, PUPIL), jnp.int32),
        V((PUPIL + HALO, PUPIL), BF16),
        V((PUPIL, PUPIL), BF16),
        V((4, BLOCK, 256), BF16),
        V((PUPIL, 256), BF16),
        V((2, FOCAL, LANES), BF16),
        V((HALO, PUPIL), BF16),
        V((HALO, PUPIL), BF16),
        V((2, PUPIL), F32),
        V((2, PUPIL), F32),
        V((Y, 2, 2, LANES), jnp.int32),
        V((Z, 2, LANES), jnp.int32),
        V((PUPIL, 256), BF16),
        V((X, WINDOW, 256), BF16),
        V((X, WINDOW, 256), BF16),
        V((2, WINDOW, PUPIL), F32),
        V((2, WINDOW, PUPIL), F32),
        V((2, Y, PR, LANES), F32),
        V((2, Y, PR, LANES), F32),
        V((Y, PR, LANES), F32),
        V((Y, PR, LANES), F32),
        V((Z, PR, LANES), F32),
        V((Y, PR16, LANES), BF16),
        V((2, Y, PR16, LANES), BF16),
        V((WINDOW, PUPIL), F32),
        V((2, 2, WINDOW, PUPIL), F32),
        V((2, WINDOW, PUPIL), F32),
        V((2, Y, 2, PR, LANES), F32),
        V((Y, 2, PR, LANES), F32),
        V((Y, 2, PR, LANES), F32),
        V((Y, 2, PR, LANES), F32),
        V((Z, X, 2, LANES), F32),
        V((2 * Y, 2, LANES), F32),
        V((2, BLOCK, PUPIL), F32),
        pltpu.SemaphoreType.DMA((6,)),
        pltpu.SemaphoreType.DMA((2,)),
        sems(X), sems(X), sems(2), sems(2 * Y), sems(Z), sems(X), sems(2), sems(Y), sems(Z), sems(Y),
        sems(1), sems(1), sems(Y), sems(X * Z), sems(2 * Y), sems(1), pltpu.SemaphoreType.REGULAR((2,)),
    ]
    shapes = (
        jax.ShapeDtypeStruct((2, BLOCK, PUPIL), F32),
        jax.ShapeDtypeStruct((2,), F32),
    )
    return pl.pallas_call(
        functools.partial(body, Y, Z, X),
        name="adjoint_sweep",
        out_shape=shapes,
        in_specs=[hbm] * 6,
        out_specs=(hbm, smem),
        scratch_shapes=scratch,
        compiler_params=pltpu.CompilerParams(
            collective_id=1, has_side_effects=True, vmem_limit_bytes=63 << 20
        ),
    )(phases, focal, shifts, mask, jnp.asarray(by_pupil), jnp.asarray(by_focal))


def solution(mesh):
    X = mesh.shape["rows"]
    count = mesh.shape["tm"]
    Y = 8 if count == 128 else 2
    Z = count // (2 * Y)
    in_specs = (P("tm", "rows", None), P("tm", None, "rows", None), P("tm", None), P("rows", None))
    out_specs = (P("tm", "rows", None), P())
    return jax.shard_map(
        functools.partial(on_device, Y, Z, X), mesh=mesh, in_specs=in_specs, out_specs=out_specs,
        check_vma=False,
    )
```

```python
import functools
import math

import jax
import jax.numpy as jnp
import numpy as np
from jax import lax
from jax.experimental import pallas as pl
from jax.experimental.pallas import tpu as pltpu
from jax.sharding import PartitionSpec as P

PUPIL = 512
FOCAL = 256
HALO = 32
LANES = 128
DECAY = 0.999
MESH = pl.DeviceIdType.MESH
F32 = jnp.float32
BF16 = jnp.bfloat16


def transform_tables():
    focal_pos = np.arange(FOCAL, dtype=np.int32) - FOCAL // 2
    pupil_pos = np.arange(PUPIL, dtype=np.int32) - PUPIL // 2
    turns = np.mod(focal_pos[:, None] * pupil_pos[None, :], 2 * PUPIL)
    angle = turns.astype(np.float32) * np.float32(math.pi / PUPIL)
    factor = np.float32(1.0 / math.sqrt(PUPIL))
    cos_t = (np.cos(angle) * factor).astype(BF16)
    sin_t = (-np.sin(angle) * factor).astype(BF16)
    half = FOCAL // 2
    by_focal = np.concatenate([cos_t[:half], sin_t[:half], cos_t[half:], sin_t[half:]], axis=0)
    return np.ascontiguousarray(by_focal.T), by_focal


def body(
    Y, Z, X, phases_h, focal_h, shifts_h, mask_h, by_pupil_h, by_focal_h, out_h, wind,
    phases, shifts, mask, by_pupil, by_focal,
    y_send, y_recv, f_recv, h_send, h_recv, p_send, p_recv, s_recv, t_recv, resid, w_buf, w_recv,
    grad, gb, bseg, cx, ag, ys, zs, ret, cr, carry, diffs, d0b, qseg, qx, qc, qy, wz, wy, out,
    in_sem, out_sem, y_sem, f_sem, h_sem, s_sem, t_sem, w_sem, c_sem, ys_sem, zs_sem, r_sem, cr_sem,
    qx_sem, qy_sem, wz_sem, wy_sem, sc_sem, ring_sem,
):
    BLOCK = PUPIL // X
    WINDOW = BLOCK + HALO
    PIECES = 2 * Y
    PR = WINDOW * 4 // PIECES
    PR16 = -(-PR // 16) * 16
    me = lax.axis_index("tm")
    x = lax.axis_index("rows")
    core = lax.rem(me, 2)
    y = lax.rem(me // 2, Y)
    z = me // (2 * Y)
    other = 1 - core

    def at(x_=None, y_=None, z_=None, c_=None):
        zz = z if z_ is None else z_
        yy = y if y_ is None else y_
        cc = core if c_ is None else c_
        return ((zz * Y + yy) * 2 + cc, x if x_ is None else x_)

    def copy(src, dst, sems, n, device):
        return pltpu.make_async_remote_copy(
            src_ref=src, dst_ref=dst, send_sem=sems.at[0, n], recv_sem=sems.at[1, n],
            device_id=device, device_id_type=MESH,
        )

    def start(copies):
        for c in copies:
            c.start()
        return copies

    def arrive(copies):
        for c in copies:
            c.wait_recv()

    waiting = []

    def far_first(n):
        return sorted(range(1, n), key=lambda p: -min(p, n - p))

    xs = [lax.rem(x + p, X) for p in far_first(X)]
    yy = [lax.rem(y + p, Y) for p in far_first(Y)]
    zz = [lax.rem(z + p, Z) for p in far_first(Z)]
    lines = [
        at(y_=lax.rem(y + p, Y), c_=lax.rem(core + q, 2))
        for p in far_first(Y) for q in range(2)
    ] + [at(c_=other)]

    zs[...] = jnp.zeros((Z, PR, LANES), F32)
    def ring(d):
        near_y = [at(y_=lax.rem(y + p, Y)) for p in sorted({d % Y, -d % Y} - {0})]
        return near_y + [at(z_=lax.rem(z + p, Z)) for p in sorted({d % Z, -d % Z} - {0})]

    relayed = max(Y, Z) > 5

    barrier = pltpu.get_barrier_semaphore()
    entry = [at(x_=k) for k in xs] + ring(2) + ring(1) + [at(c_=other)]
    for dev in entry:
        pl.semaphore_signal(barrier, inc=1, device_id=dev, device_id_type=MESH)
    q_rows = FOCAL // X
    q_of = lambda k: pl.ds(pl.multiple_of(k * q_rows, q_rows), q_rows)
    cols_of = lambda k: pl.ds(pl.multiple_of(lax.rem(k, 2) * LANES, LANES), LANES)
    loads = [
        pltpu.make_async_copy(src, dst, in_sem.at[n])
        for n, (src, dst) in enumerate([
            (shifts_h, shifts),
            (phases_h, phases),
            (mask_h, mask),
            (by_pupil_h, by_pupil.at[0:PUPIL]),
            (by_focal_h, by_focal),
            (focal_h.at[x // 2, :, :, cols_of(x)], f_recv.at[:, q_of(x), :]),
        ])
    ]
    for load in loads:
        load.start()

    for load in loads[0:3]:
        load.wait()
    a0, b0, a1, b1 = shifts[0, 0], shifts[0, 1], shifts[1, 0], shifts[1, 1]
    live = jnp.where(mask[...] == 1, 1.0, 0.0).astype(F32)
    h_send[0:HALO] = live[0:HALO].astype(BF16)
    for f in range(2):
        p_send[f : f + 1] = phases[f, 0:16].astype(F32)[0:1]
    my_line = y * 2 + core
    s_recv[y, core, 0:1] = jnp.full((1, LANES), a0 + a1, jnp.int32)
    s_recv[y, core, 1:2] = jnp.full((1, LANES), b0 + b1, jnp.int32)
    pl.semaphore_wait(barrier, len(entry))
    if relayed:
        for dev in ring(2):
            pl.semaphore_signal(ring_sem, inc=1, device_id=dev, device_id_type=MESH)
    sc_copies = start([copy(s_recv.at[y, core], s_recv.at[y, core], sc_sem, 0, at(c_=other))])
    waiting += sc_copies
    loads[3].wait()
    for f in range(2):
        masked = (phases[f].astype(F32) * live).astype(BF16)
        yv = jnp.dot(masked, by_pupil[0:PUPIL], preferred_element_type=F32).astype(BF16)
        y_send[2 * f] = yv[:, 0:256]
        y_send[2 * f + 1] = yv[:, 256:512]


    rows_of = lambda k: pl.ds(pl.multiple_of(k * BLOCK, BLOCK), BLOCK)
    y_copies = start([
        copy(y_send.at[k], y_recv.at[rows_of(x)], y_sem, n, at(x_=k)) for n, k in enumerate(xs)
    ])
    f_copies = start([
        copy(focal_h.at[k // 2, :, :, cols_of(k)], f_recv.at[:, q_of(x), :], f_sem, n, at(x_=k))
        for n, k in enumerate(xs)
    ])
    above = at(x_=lax.rem(x + X - 1, X))
    h_copies = start([
        copy(p_send, p_recv, h_sem, 0, above), copy(h_send, h_recv, h_sem, 1, above)
    ])
    waiting += y_copies + f_copies + h_copies
    if relayed:
        pl.semaphore_wait(ring_sem, len(ring(2)))
    arrive(sc_copies)
    s_copies = start([
        copy(s_recv.at[y], s_recv.at[y], s_sem, n, at(y_=k)) for n, k in enumerate(yy)
    ])
    waiting += s_copies

    y_recv[rows_of(x)] = y_send[x]
    by_pupil[PUPIL : PUPIL + HALO] = jnp.zeros((HALO, PUPIL), BF16)
    if PR16 > PR:
        ret[:, PR:PR16] = jnp.zeros((Y, PR16 - PR, LANES), BF16)

    arrive(y_copies)
    loads[4].wait()
    m = jnp.dot(by_focal[...], y_recv[...], preferred_element_type=F32)
    loads[5].wait()
    arrive(f_copies)
    for h in range(2):
        mc, ms = m[256 * h : 256 * h + 128], m[256 * h + 128 : 256 * h + 256]
        e_real = mc[:, 0:128] - ms[:, 128:256]
        e_imag = mc[:, 128:256] + ms[:, 0:128]
        r_real = (f_recv[0, 128 * h : 128 * h + 128].astype(F32) - e_real).astype(BF16)
        r_imag = (f_recv[1, 128 * h : 128 * h + 128].astype(F32) - e_imag).astype(BF16)
        resid[256 * h : 256 * h + 128, 0:128] = r_real
        resid[256 * h : 256 * h + 128, 128:256] = r_imag
        resid[256 * h + 128 : 256 * h + 256, 0:128] = r_imag
        resid[256 * h + 128 : 256 * h + 256, 128:256] = -r_real
    win_of = lambda k: pl.ds(pl.multiple_of(k * BLOCK, BLOCK), WINDOW)
    w_copies = []
    for n, k in enumerate(xs + [x]):
        rows = jnp.dot(by_pupil[win_of(k)], resid[...], preferred_element_type=F32)
        if n == X - 1:
            w_recv[x] = rows.astype(BF16)
        else:
            w_buf[n] = rows.astype(BF16)
            w_copies += start([copy(w_buf.at[n], w_recv.at[x], w_sem, n, at(x_=k))])
    waiting += w_copies

    arrive(s_copies)
    total_shift = jnp.zeros((2, LANES), jnp.int32)
    for k in range(Y):
        for c in range(2):
            total_shift = total_shift + s_recv[k, c]
    t_recv[z] = total_shift
    t_copies = start([
        copy(t_recv.at[z], t_recv.at[z], t_sem, n, at(z_=k)) for n, k in enumerate(zz)
    ])
    waiting += t_copies

    lane = lax.broadcasted_iota(jnp.int32, (1, LANES), 1)
    wide = lax.broadcasted_iota(jnp.int32, (1, PUPIL), 1)

    arrive(h_copies)
    inner = jnp.where(x < X - 1, 1.0, 0.0).astype(F32)
    for f in range(2):
        now = phases[f].astype(F32)
        below = p_recv[f : f + 1] * inner
        diffs[f, 0, 0:BLOCK] = jnp.concatenate([now[1:], below], axis=0) - now
        diffs[f, 1, 0:BLOCK] = jnp.where(wide == PUPIL - 1, 0.0, pltpu.roll(now, PUPIL - 1, 1)) - now
        for n in range(2):
            diffs[f, n, BLOCK:WINDOW] = jnp.zeros((HALO, PUPIL), F32)
    arrive(w_copies)
    for f in range(2):
        g = jnp.dot(w_recv[2 * f], by_focal[0:256], preferred_element_type=F32) + jnp.dot(
            w_recv[2 * f + 1], by_focal[256:512], preferred_element_type=F32
        )
        grad[f, 0:BLOCK] = g[0:BLOCK] * live
        grad[f, BLOCK:WINDOW] = g[BLOCK:WINDOW] * h_recv[0:HALO].astype(F32)
    arrive(t_copies)
    zero_tile = jnp.zeros((2, LANES), jnp.int32)
    beyond = zero_tile
    z_cols = [None] * Z + [zero_tile[1:2]]
    for k in reversed(range(Z)):
        beyond = beyond + jnp.where(k > z, t_recv[k], zero_tile)
        z_cols[k] = z_cols[k + 1] + t_recv[k, 1:2]
    chip_end = beyond[1:2]
    y_cols = [None] * Y + [chip_end]
    own_sum, c0_sum, c1_sum, c2_sum = beyond, beyond, beyond, beyond
    for k in reversed(range(Y)):
        y_cols[k] = y_cols[k + 1] + s_recv[k, 1, 1:2] + s_recv[k, 0, 1:2]
        for c in range(2):
            line = 2 * k + c
            tile = s_recv[k, c]
            own_sum = own_sum + jnp.where(line >= my_line, tile, zero_tile)
            c0_sum = c0_sum + jnp.where(line >= 2 * y, tile, zero_tile)
            c1_sum = c1_sum + jnp.where(line >= 2 * y + 1, tile, zero_tile)
            c2_sum = c2_sum + jnp.where(line >= 2 * y + 2, tile, zero_tile)
    row0 = jnp.max(own_sum[0:1])
    row1 = row0 - a0
    col0 = jnp.max(own_sum[1:2])
    col1 = col0 - b0
    col2 = col1 - b1
    chip_col0, chip_col1, chip_col2 = c0_sum[1:2], c1_sum[1:2], c2_sum[1:2]

    def keep(cols, late, early):
        return jnp.where(((cols - late) & (PUPIL - 1)) >= early - late, 1.0, 0.0).astype(F32)

    def block_cols(piece):
        return lax.rem(piece, 4) * LANES + lane

    def rows_cols(piece):
        r, c = piece // 4, piece % 4
        return slice(PR * r, PR * r + PR), slice(LANES * c, LANES * c + LANES)

    def shifted(value, f):
        turned = pltpu.roll(value, (row0, row1)[f], 0)
        return pltpu.roll(turned, (col0, col1)[f] & (PUPIL - 1), 1)

    def folded(value):
        parts = jnp.sum(value.reshape(value.shape[0] // 8, 8, value.shape[1]), axis=0)
        total = parts[:, 0:LANES]
        for c in range(1, value.shape[1] // LANES):
            total = total + parts[:, LANES * c : LANES * c + LANES]
        return total

    keep_01 = DECAY * keep(wide, col1, col0)
    keep_12 = DECAY * keep(wide, col2, col1)
    for f in range(2):
        gb[f] = shifted(grad[f], f)
    seg = gb[0] + gb[1] * keep_01

    for m_ in range(PIECES):
        r, c = rows_cols(m_)
        bseg[m_ % 2, m_ // 2] = seg[r, c]

    c_copies = start([
        copy(bseg.at[other], cx.at[other], c_sem, 0, at(c_=other)),
        copy(bseg.at[core], cx.at[core], c_sem, 1, at(c_=other)),
    ])
    waiting += c_copies
    for n in range(2):
        d0b[n] = keep_01 * shifted(diffs[0, n], 0)
        weight = keep_12 * (shifted(diffs[1, n], 1) + d0b[n])
        for m_ in range(PIECES):
            r, c = rows_cols(m_)
            qseg[m_ % 2, m_ // 2, n] = weight[r, c]
    qx_copies = start([copy(qseg.at[other], qx, qx_sem, 0, at(c_=other))])
    waiting += qx_copies
    arrive(c_copies[0:1])
    first = core == 0
    for k in range(Y):
        mine, theirs = bseg[core, k], cx[core, k]
        early = jnp.where(first, mine, theirs)
        late = jnp.where(first, theirs, mine)
        ag[k] = early + late * (DECAY**2 * keep(block_cols(2 * k + core), chip_col1, chip_col0))
    ys_copies = start([
        copy(ag.at[k], ys.at[y], ys_sem, n, at(y_=k)) for n, k in enumerate(yy)
    ])
    waiting += ys_copies
    ys[y] = ag[y]
    arrive(qx_copies)
    tiles = [folded(gb[1] * d0b[n]) for n in range(2)]
    for k in range(Y):
        late = jnp.where(first, cx[core, k], bseg[core, k])
        keep_k = DECAY**2 * keep(block_cols(2 * k + core), chip_col2, chip_col1)
        for n in range(2):
            mine, theirs = qseg[core, k, n], qx[k, n]
            early_q = jnp.where(first, mine, theirs)
            late_q = jnp.where(first, theirs, mine)
            tiles[n] = tiles[n] + folded(late * early_q)
            qc[k, n] = late_q + keep_k * early_q
    qy_copies = start([
        copy(qc.at[k], qy.at[y], qy_sem, n, at(y_=k)) for n, k in enumerate(yy)
    ])
    waiting += qy_copies
    qy[y] = qc[y]
    arrive(ys_copies)
    my_cols = block_cols(my_line)
    later = [None] * Y
    later[Y - 1] = jnp.zeros((PR, LANES), F32)
    for k in reversed(range(Y - 1)):
        later[k] = ys[k + 1] + later[k + 1] * (DECAY**4 * keep(my_cols, y_cols[k + 2], y_cols[k + 1]))
    zs[z] = ys[0] + later[0] * (DECAY**4 * keep(my_cols, y_cols[1], y_cols[0]))
    zs_copies = [copy(zs.at[z], zs.at[z], zs_sem, n, at(z_=k)) for n, k in enumerate(zz)]
    for n, k in enumerate(zz):
        pl.when(k < z)(zs_copies[n].start)
    reach = [
        DECAY ** (4 * (Y - 1 - k)) * keep(my_cols, chip_end, y_cols[k + 1]) for k in range(Y)
    ]
    arrive(qy_copies)
    whole = [jnp.zeros((PR, LANES), F32) for _ in range(2)]
    for k in range(Y):
        for n in range(2):
            tiles[n] = tiles[n] + folded(later[k] * qy[k, n])
            whole[n] = whole[n] + reach[k] * qy[k, n]
    for n, p in enumerate(far_first(Z)):
        pl.when(lax.rem(z + Z - p, Z) > z)(zs_copies[n].wait_recv)
    acc = jnp.zeros((PR, LANES), F32)
    for k in reversed(range(1, Z)):
        new = zs[k] + acc * (DECAY ** (4 * Y) * keep(my_cols, z_cols[k + 1], z_cols[k]))
        acc = jnp.where(k > z, new, acc)
    for k in range(Y):
        ret[k, 0:PR] = (later[k] + acc * reach[k]).astype(BF16)
    r_copies = start([
        copy(ret.at[k], cr.at[core, y], r_sem, n, at(y_=k)) for n, k in enumerate(yy)
    ])
    waiting += r_copies
    cr[core, y] = ret[y]

    for n in range(2):
        wz[z, x, n : n + 1] = jnp.sum(tiles[n] + folded(acc * whole[n]), axis=0, keepdims=True)
    cross = sorted(
        ((p, q) for p in range(Z) for q in range(X) if p or q),
        key=lambda t: -min(t[0], Z - t[0]) - min(t[1], X - t[1]),
    )
    wz_copies = start([
        copy(wz.at[z, x], wz.at[z, x], wz_sem, n, at(z_=lax.rem(z + p, Z), x_=lax.rem(x + q, X)))
        for n, (p, q) in enumerate(cross)
    ])
    waiting += wz_copies
    arrive(wz_copies)
    sums = jnp.zeros((2, LANES), F32)
    for k in range(Z):
        for q in range(X):
            sums = sums + wz[k, q]
    wy[my_line] = sums
    wy_copies = start([
        copy(wy.at[my_line], wy.at[my_line], wy_sem, n, dev) for n, dev in enumerate(lines)
    ])
    waiting += wy_copies
    arrive(r_copies)
    cr_copies = start([copy(cr.at[core], cr.at[core], cr_sem, 0, at(c_=other))])
    waiting += cr_copies
    arrive(c_copies[1:2])
    arrive(cr_copies)
    for m_ in range(PIECES):
        r, c = rows_cols(m_)
        chip = cr[m_ % 2, m_ // 2].astype(F32)[0:PR]
        within = cx[m_ % 2, m_ // 2] + chip * (
            DECAY**2 * keep(block_cols(m_), chip_col2, chip_col1)
        )
        carry[r, c] = jnp.where(first, within, chip)

    prior_b = carry[...] * keep_12
    stores = []
    for f in (1, 0):
        moved = pltpu.roll(prior_b, lax.rem(WINDOW - (row0, row1)[f], WINDOW), 0)[0:BLOCK]
        prior = pltpu.roll(moved, (PUPIL - (col0, col1)[f]) & (PUPIL - 1), 1)
        out[f] = grad[f, 0:BLOCK] + prior
        stores.append(pltpu.make_async_copy(out.at[f], out_h.at[f], out_sem.at[f]))
        stores[-1].start()
        if f == 1:
            prior_b = (gb[1] + prior_b) * keep_01

    arrive(wy_copies)
    total = wy[0]
    for k in range(1, 2 * Y):
        total = total + wy[k]
    scale = -1.0 / (PUPIL * 2.0 * 2 * Y * Z)
    wind[0] = jnp.sum(total[0:1]) * scale
    wind[1] = jnp.sum(total[1:2]) * scale
    for n, k in enumerate(zz):
        pl.when(k < z)(zs_copies[n].wait_send)
    for store in stores:
        store.wait()
    for c in waiting:
        c.wait_send()


def finish(field_h, sums, out_h, wind, held, sem_in, sem_out):
    parts = sem_in.shape[0] // field_h.shape[0]
    rows = field_h.shape[1] // parts
    places = [(f, pl.ds(p * rows, rows)) for f in range(field_h.shape[0]) for p in range(parts)]
    loads = [
        pltpu.make_async_copy(field_h.at[here], held.at[here], sem_in.at[n])
        for n, here in enumerate(places)
    ]
    stores = [
        pltpu.make_async_copy(held.at[here], out_h.at[here], sem_out.at[n])
        for n, here in enumerate(places)
    ]
    for load in loads:
        load.start()
    wind[0] = sums[0]
    wind[1] = sums[1]
    for load, store in zip(loads, stores):
        load.wait()
        store.start()
    for store in stores:
        store.wait()


def on_device(Y, Z, X, phases, focal, shifts, mask):
    BLOCK = PUPIL // X
    WINDOW = BLOCK + HALO
    PIECES = 2 * Y
    PR = WINDOW * 4 // PIECES
    PR16 = -(-PR // 16) * 16
    by_pupil, by_focal = transform_tables()
    smem = pl.BlockSpec(memory_space=pltpu.SMEM)
    hbm = pl.BlockSpec(memory_space=pltpu.HBM)
    V = pltpu.VMEM

    def sems(n):
        return pltpu.SemaphoreType.DMA((2, n))

    scratch = [
        V((2, BLOCK, PUPIL), BF16),
        pltpu.SMEM((2, 2), jnp.int32),
        V((BLOCK, PUPIL), jnp.int32),
        V((PUPIL + HALO, PUPIL), BF16),
        V((PUPIL, PUPIL), BF16),
        V((4, BLOCK, 256), BF16),
        V((PUPIL, 256), BF16),
        V((2, FOCAL, LANES), BF16),
        V((HALO, PUPIL), BF16),
        V((HALO, PUPIL), BF16),
        V((2, PUPIL), F32),
        V((2, PUPIL), F32),
        V((Y, 2, 2, LANES), jnp.int32),
        V((Z, 2, LANES), jnp.int32),
        V((PUPIL, 256), BF16),
        V((X, WINDOW, 256), BF16),
        V((X, WINDOW, 256), BF16),
        V((2, WINDOW, PUPIL), F32),
        V((2, WINDOW, PUPIL), F32),
        V((2, Y, PR, LANES), F32),
        V((2, Y, PR, LANES), F32),
        V((Y, PR, LANES), F32),
        V((Y, PR, LANES), F32),
        V((Z, PR, LANES), F32),
        V((Y, PR16, LANES), BF16),
        V((2, Y, PR16, LANES), BF16),
        V((WINDOW, PUPIL), F32),
        V((2, 2, WINDOW, PUPIL), F32),
        V((2, WINDOW, PUPIL), F32),
        V((2, Y, 2, PR, LANES), F32),
        V((Y, 2, PR, LANES), F32),
        V((Y, 2, PR, LANES), F32),
        V((Y, 2, PR, LANES), F32),
        V((Z, X, 2, LANES), F32),
        V((2 * Y, 2, LANES), F32),
        V((2, BLOCK, PUPIL), F32),
        pltpu.SemaphoreType.DMA((6,)),
        pltpu.SemaphoreType.DMA((2,)),
        sems(X), sems(X), sems(2), sems(2 * Y), sems(Z), sems(X), sems(2), sems(Y), sems(Z), sems(Y),
        sems(1), sems(1), sems(Y), sems(X * Z), sems(2 * Y), sems(1), pltpu.SemaphoreType.REGULAR,
    ]
    shapes = (
        jax.ShapeDtypeStruct((2, BLOCK, PUPIL), F32),
        jax.ShapeDtypeStruct((2,), F32),
    )
    field, sums = pl.pallas_call(
        functools.partial(body, Y, Z, X),
        name="adjoint_sweep",
        out_shape=shapes,
        in_specs=[hbm] * 6,
        out_specs=(hbm, smem),
        scratch_shapes=scratch,
        compiler_params=pltpu.CompilerParams(
            collective_id=1, has_side_effects=True, vmem_limit_bytes=63 << 20
        ),
    )(phases, focal, shifts, mask, jnp.asarray(by_pupil), jnp.asarray(by_focal))
    return pl.pallas_call(
        finish,
        name="finish",
        out_shape=shapes,
        in_specs=[hbm, smem],
        out_specs=(hbm, smem),
        scratch_shapes=[
            V((2, BLOCK, PUPIL), F32),
            pltpu.SemaphoreType.DMA((4,)),
            pltpu.SemaphoreType.DMA((4,)),
        ],
        compiler_params=pltpu.CompilerParams(vmem_limit_bytes=63 << 20),
    )(field, sums)


def solution(mesh):
    X = mesh.shape["rows"]
    count = mesh.shape["tm"]
    Y = 8 if count == 128 else 2
    Z = count // (2 * Y)
    in_specs = (P("tm", "rows", None), P("tm", None, "rows", None), P("tm", None), P("rows", None))
    out_specs = (P("tm", "rows", None), P())
    return jax.shard_map(
        functools.partial(on_device, Y, Z, X), mesh=mesh, in_specs=in_specs, out_specs=out_specs,
        check_vma=False,
    )
```

```python
import functools
import math

import jax
import jax.numpy as jnp
import numpy as np
from jax import lax
from jax.experimental import pallas as pl
from jax.experimental.pallas import tpu as pltpu
from jax.sharding import PartitionSpec as P

PUPIL = 512
FOCAL = 256
HALO = 32
LANES = 128
DECAY = 0.999
MESH = pl.DeviceIdType.MESH
F32 = jnp.float32
BF16 = jnp.bfloat16


def transform_tables():
    focal_pos = np.arange(FOCAL, dtype=np.int32) - FOCAL // 2
    pupil_pos = np.arange(PUPIL, dtype=np.int32) - PUPIL // 2
    turns = np.mod(focal_pos[:, None] * pupil_pos[None, :], 2 * PUPIL)
    angle = turns.astype(np.float32) * np.float32(math.pi / PUPIL)
    factor = np.float32(1.0 / math.sqrt(PUPIL))
    cos_t = (np.cos(angle) * factor).astype(BF16)
    sin_t = (-np.sin(angle) * factor).astype(BF16)
    half = FOCAL // 2
    by_focal = np.concatenate([cos_t[:half], sin_t[:half], cos_t[half:], sin_t[half:]], axis=0)
    return np.ascontiguousarray(by_focal.T), by_focal


def body(
    Y, Z, X, phases_h, focal_h, shifts_h, mask_h, by_pupil_h, by_focal_h, out_h, wind,
    phases, shifts, mask, by_pupil, by_focal,
    y_send, y_recv, f_recv, h_send, h_recv, p_send, p_recv, s_recv, t_recv, resid, w_buf, w_recv,
    grad, gb, bseg, cx, ag, ys, zs, ret, cr, carry, wide_ph, d0b, qseg, qx, qc, qy, wz, wy, out,
    in_sem, out_sem, y_sem, f_sem, h_sem, s_sem, t_sem, w_sem, c_sem, ys_sem, zs_sem, r_sem, cr_sem,
    qx_sem, qy_sem, wz_sem, wy_sem, sc_sem, ring_sem,
):
    BLOCK = PUPIL // X
    WINDOW = BLOCK + HALO
    PIECES = 2 * Y
    PR = WINDOW * 4 // PIECES
    PR16 = -(-PR // 16) * 16
    me = lax.axis_index("tm")
    x = lax.axis_index("rows")
    core = lax.rem(me, 2)
    y = lax.rem(me // 2, Y)
    z = me // (2 * Y)
    other = 1 - core

    def at(x_=None, y_=None, z_=None, c_=None):
        zz = z if z_ is None else z_
        yy = y if y_ is None else y_
        cc = core if c_ is None else c_
        return ((zz * Y + yy) * 2 + cc, x if x_ is None else x_)

    def copy(src, dst, sems, n, device):
        return pltpu.make_async_remote_copy(
            src_ref=src, dst_ref=dst, send_sem=sems.at[0, n], recv_sem=sems.at[1, n],
            device_id=device, device_id_type=MESH,
        )

    def start(copies):
        for c in copies:
            c.start()
        return copies

    def arrive(copies):
        for c in copies:
            c.wait_recv()

    waiting = []

    def far_first(n):
        return sorted(range(1, n), key=lambda p: -min(p, n - p))

    xs = [lax.rem(x + p, X) for p in far_first(X)]
    yy = [lax.rem(y + p, Y) for p in far_first(Y)]
    zz = [lax.rem(z + p, Z) for p in far_first(Z)]
    lines = [
        at(y_=lax.rem(y + p, Y), c_=lax.rem(core + q, 2))
        for p in far_first(Y) for q in range(2)
    ] + [at(c_=other)]

    zs[...] = jnp.zeros((Z, PR, LANES), F32)
    def ring(d):
        near_y = [at(y_=lax.rem(y + p, Y)) for p in sorted({d % Y, -d % Y} - {0})]
        return near_y + [at(z_=lax.rem(z + p, Z)) for p in sorted({d % Z, -d % Z} - {0})]

    relayed = max(Y, Z) > 5

    barrier = pltpu.get_barrier_semaphore()
    entry = [at(x_=k) for k in xs] + ring(2) + ring(1) + [at(c_=other)]
    for dev in entry:
        pl.semaphore_signal(barrier, inc=1, device_id=dev, device_id_type=MESH)
    q_rows = FOCAL // X
    q_of = lambda k: pl.ds(pl.multiple_of(k * q_rows, q_rows), q_rows)
    cols_of = lambda k: pl.ds(pl.multiple_of(lax.rem(k, 2) * LANES, LANES), LANES)
    loads = [
        pltpu.make_async_copy(src, dst, in_sem.at[n])
        for n, (src, dst) in enumerate([
            (shifts_h, shifts),
            (phases_h, phases),
            (mask_h, mask),
            (by_pupil_h, by_pupil.at[0:PUPIL]),
            (by_focal_h, by_focal),
            (focal_h.at[x // 2, :, :, cols_of(x)], f_recv.at[:, q_of(x), :]),
        ])
    ]
    for load in loads:
        load.start()

    for load in loads[0:3]:
        load.wait()
    a0, b0, a1, b1 = shifts[0, 0], shifts[0, 1], shifts[1, 0], shifts[1, 1]
    live = jnp.where(mask[...] == 1, 1.0, 0.0).astype(F32)
    h_send[0:HALO] = live[0:HALO].astype(BF16)
    for f in range(2):
        p_send[f : f + 1] = phases[f, 0:16].astype(F32)[0:1]
    my_line = y * 2 + core
    s_recv[y, core, 0:1] = jnp.full((1, LANES), a0 + a1, jnp.int32)
    s_recv[y, core, 1:2] = jnp.full((1, LANES), b0 + b1, jnp.int32)
    pl.semaphore_wait(barrier, len(entry))
    if relayed:
        for dev in ring(2):
            pl.semaphore_signal(ring_sem, inc=1, device_id=dev, device_id_type=MESH)
    sc_copies = start([copy(s_recv.at[y, core], s_recv.at[y, core], sc_sem, 0, at(c_=other))])
    waiting += sc_copies
    loads[3].wait()
    for f in range(2):
        masked = (phases[f].astype(F32) * live).astype(BF16)
        yv = jnp.dot(masked, by_pupil[0:PUPIL], preferred_element_type=F32).astype(BF16)
        y_send[2 * f] = yv[:, 0:256]
        y_send[2 * f + 1] = yv[:, 256:512]


    rows_of = lambda k: pl.ds(pl.multiple_of(k * BLOCK, BLOCK), BLOCK)
    y_copies = start([
        copy(y_send.at[k], y_recv.at[rows_of(x)], y_sem, n, at(x_=k)) for n, k in enumerate(xs)
    ])
    f_copies = start([
        copy(focal_h.at[k // 2, :, :, cols_of(k)], f_recv.at[:, q_of(x), :], f_sem, n, at(x_=k))
        for n, k in enumerate(xs)
    ])
    above = at(x_=lax.rem(x + X - 1, X))
    h_copies = start([
        copy(p_send, p_recv, h_sem, 0, above), copy(h_send, h_recv, h_sem, 1, above)
    ])
    waiting += y_copies + f_copies + h_copies
    if relayed:
        pl.semaphore_wait(ring_sem, len(ring(2)))
    arrive(sc_copies)
    s_copies = start([
        copy(s_recv.at[y], s_recv.at[y], s_sem, n, at(y_=k)) for n, k in enumerate(yy)
    ])
    waiting += s_copies

    y_recv[rows_of(x)] = y_send[x]
    by_pupil[PUPIL : PUPIL + HALO] = jnp.zeros((HALO, PUPIL), BF16)
    if PR16 > PR:
        ret[:, PR:PR16] = jnp.zeros((Y, PR16 - PR, LANES), BF16)

    arrive(y_copies)
    loads[4].wait()
    m = jnp.dot(by_focal[...], y_recv[...], preferred_element_type=F32)
    loads[5].wait()
    arrive(f_copies)
    for h in range(2):
        mc, ms = m[256 * h : 256 * h + 128], m[256 * h + 128 : 256 * h + 256]
        e_real = mc[:, 0:128] - ms[:, 128:256]
        e_imag = mc[:, 128:256] + ms[:, 0:128]
        r_real = (f_recv[0, 128 * h : 128 * h + 128].astype(F32) - e_real).astype(BF16)
        r_imag = (f_recv[1, 128 * h : 128 * h + 128].astype(F32) - e_imag).astype(BF16)
        resid[256 * h : 256 * h + 128, 0:128] = r_real
        resid[256 * h : 256 * h + 128, 128:256] = r_imag
        resid[256 * h + 128 : 256 * h + 256, 0:128] = r_imag
        resid[256 * h + 128 : 256 * h + 256, 128:256] = -r_real
    win_of = lambda k: pl.ds(pl.multiple_of(k * BLOCK, BLOCK), WINDOW)
    w_copies = []
    for n, k in enumerate(xs + [x]):
        rows = jnp.dot(by_pupil[win_of(k)], resid[...], preferred_element_type=F32)
        if n == X - 1:
            w_recv[x] = rows.astype(BF16)
        else:
            w_buf[n] = rows.astype(BF16)
            w_copies += start([copy(w_buf.at[n], w_recv.at[x], w_sem, n, at(x_=k))])
    waiting += w_copies

    arrive(s_copies)
    total_shift = jnp.zeros((2, LANES), jnp.int32)
    for k in range(Y):
        for c in range(2):
            total_shift = total_shift + s_recv[k, c]
    t_recv[z] = total_shift
    t_copies = start([
        copy(t_recv.at[z], t_recv.at[z], t_sem, n, at(z_=k)) for n, k in enumerate(zz)
    ])
    waiting += t_copies

    lane = lax.broadcasted_iota(jnp.int32, (1, LANES), 1)
    wide = lax.broadcasted_iota(jnp.int32, (1, PUPIL), 1)

    arrive(h_copies)
    inner = jnp.where(x < X - 1, 1.0, 0.0).astype(F32)
    for f in range(2):
        wide_ph[f, 0:BLOCK] = phases[f].astype(F32)
        wide_ph[f, BLOCK:WINDOW] = jnp.zeros((HALO, PUPIL), F32)
        wide_ph[f, BLOCK : BLOCK + 1] = p_recv[f : f + 1] * inner
    arrive(w_copies)
    for f in range(2):
        g = jnp.dot(w_recv[2 * f], by_focal[0:256], preferred_element_type=F32) + jnp.dot(
            w_recv[2 * f + 1], by_focal[256:512], preferred_element_type=F32
        )
        grad[f, 0:BLOCK] = g[0:BLOCK] * live
        grad[f, BLOCK:WINDOW] = g[BLOCK:WINDOW] * h_recv[0:HALO].astype(F32)
    arrive(t_copies)
    zero_tile = jnp.zeros((2, LANES), jnp.int32)
    beyond = zero_tile
    z_cols = [None] * Z + [zero_tile[1:2]]
    for k in reversed(range(Z)):
        beyond = beyond + jnp.where(k > z, t_recv[k], zero_tile)
        z_cols[k] = z_cols[k + 1] + t_recv[k, 1:2]
    chip_end = beyond[1:2]
    y_cols = [None] * Y + [chip_end]
    own_sum, c0_sum, c1_sum, c2_sum = beyond, beyond, beyond, beyond
    for k in reversed(range(Y)):
        y_cols[k] = y_cols[k + 1] + s_recv[k, 1, 1:2] + s_recv[k, 0, 1:2]
        for c in range(2):
            line = 2 * k + c
            tile = s_recv[k, c]
            own_sum = own_sum + jnp.where(line >= my_line, tile, zero_tile)
            c0_sum = c0_sum + jnp.where(line >= 2 * y, tile, zero_tile)
            c1_sum = c1_sum + jnp.where(line >= 2 * y + 1, tile, zero_tile)
            c2_sum = c2_sum + jnp.where(line >= 2 * y + 2, tile, zero_tile)
    row0 = jnp.max(own_sum[0:1])
    row1 = row0 - a0
    col0 = jnp.max(own_sum[1:2])
    col1 = col0 - b0
    col2 = col1 - b1
    chip_col0, chip_col1, chip_col2 = c0_sum[1:2], c1_sum[1:2], c2_sum[1:2]

    def keep(cols, late, early):
        return jnp.where(((cols - late) & (PUPIL - 1)) >= early - late, 1.0, 0.0).astype(F32)

    def block_cols(piece):
        return lax.rem(piece, 4) * LANES + lane

    def rows_cols(piece):
        r, c = piece // 4, piece % 4
        return slice(PR * r, PR * r + PR), slice(LANES * c, LANES * c + LANES)

    def shifted(value, f):
        turned = pltpu.roll(value, (row0, row1)[f], 0)
        return pltpu.roll(turned, (col0, col1)[f] & (PUPIL - 1), 1)

    def folded(value):
        parts = jnp.sum(value.reshape(value.shape[0] // 8, 8, value.shape[1]), axis=0)
        total = parts[:, 0:LANES]
        for c in range(1, value.shape[1] // LANES):
            total = total + parts[:, LANES * c : LANES * c + LANES]
        return total

    keep_01 = DECAY * keep(wide, col1, col0)
    keep_12 = DECAY * keep(wide, col2, col1)
    for f in range(2):
        gb[f] = shifted(grad[f], f)
    seg = gb[0] + gb[1] * keep_01

    for m_ in range(PIECES):
        r, c = rows_cols(m_)
        bseg[m_ % 2, m_ // 2] = seg[r, c]

    c_copies = start([
        copy(bseg.at[other], cx.at[other], c_sem, 0, at(c_=other)),
        copy(bseg.at[core], cx.at[core], c_sem, 1, at(c_=other)),
    ])
    waiting += c_copies
    row_at = lax.broadcasted_iota(jnp.int32, (WINDOW, 1), 0)
    steps = []
    for f in range(2):
        placed = shifted(wide_ph[f], f)
        row = row_at - (row0, row1)[f]
        inside = jnp.where((row >= 0) & (row < BLOCK), 1.0, 0.0).astype(F32)
        last = wide == ((PUPIL - 1 + (col0, col1)[f]) & (PUPIL - 1))
        down = (pltpu.roll(placed, WINDOW - 1, 0) - placed) * inside
        side = (jnp.where(last, 0.0, pltpu.roll(placed, PUPIL - 1, 1)) - placed) * inside
        steps.append((down, side))
    for n in range(2):
        d0b[n] = keep_01 * steps[0][n]
        weight = keep_12 * (steps[1][n] + d0b[n])
        for m_ in range(PIECES):
            r, c = rows_cols(m_)
            qseg[m_ % 2, m_ // 2, n] = weight[r, c]
    qx_copies = start([copy(qseg.at[other], qx, qx_sem, 0, at(c_=other))])
    waiting += qx_copies
    arrive(c_copies[0:1])
    first = core == 0
    for k in range(Y):
        mine, theirs = bseg[core, k], cx[core, k]
        early = jnp.where(first, mine, theirs)
        late = jnp.where(first, theirs, mine)
        ag[k] = early + late * (DECAY**2 * keep(block_cols(2 * k + core), chip_col1, chip_col0))
    ys_copies = start([
        copy(ag.at[k], ys.at[y], ys_sem, n, at(y_=k)) for n, k in enumerate(yy)
    ])
    waiting += ys_copies
    ys[y] = ag[y]
    arrive(qx_copies)
    tiles = [folded(gb[1] * d0b[n]) for n in range(2)]
    for k in range(Y):
        late = jnp.where(first, cx[core, k], bseg[core, k])
        keep_k = DECAY**2 * keep(block_cols(2 * k + core), chip_col2, chip_col1)
        for n in range(2):
            mine, theirs = qseg[core, k, n], qx[k, n]
            early_q = jnp.where(first, mine, theirs)
            late_q = jnp.where(first, theirs, mine)
            tiles[n] = tiles[n] + folded(late * early_q)
            qc[k, n] = late_q + keep_k * early_q
    qy_copies = start([
        copy(qc.at[k], qy.at[y], qy_sem, n, at(y_=k)) for n, k in enumerate(yy)
    ])
    waiting += qy_copies
    qy[y] = qc[y]
    arrive(ys_copies)
    my_cols = block_cols(my_line)
    later = [None] * Y
    later[Y - 1] = jnp.zeros((PR, LANES), F32)
    for k in reversed(range(Y - 1)):
        later[k] = ys[k + 1] + later[k + 1] * (DECAY**4 * keep(my_cols, y_cols[k + 2], y_cols[k + 1]))
    zs[z] = ys[0] + later[0] * (DECAY**4 * keep(my_cols, y_cols[1], y_cols[0]))
    zs_copies = [copy(zs.at[z], zs.at[z], zs_sem, n, at(z_=k)) for n, k in enumerate(zz)]
    for n, k in enumerate(zz):
        pl.when(k < z)(zs_copies[n].start)
    reach = [
        DECAY ** (4 * (Y - 1 - k)) * keep(my_cols, chip_end, y_cols[k + 1]) for k in range(Y)
    ]
    arrive(qy_copies)
    whole = [jnp.zeros((PR, LANES), F32) for _ in range(2)]
    for k in range(Y):
        for n in range(2):
            tiles[n] = tiles[n] + folded(later[k] * qy[k, n])
            whole[n] = whole[n] + reach[k] * qy[k, n]
    for n, p in enumerate(far_first(Z)):
        pl.when(lax.rem(z + Z - p, Z) > z)(zs_copies[n].wait_recv)
    acc = jnp.zeros((PR, LANES), F32)
    for k in reversed(range(1, Z)):
        new = zs[k] + acc * (DECAY ** (4 * Y) * keep(my_cols, z_cols[k + 1], z_cols[k]))
        acc = jnp.where(k > z, new, acc)
    for k in range(Y):
        ret[k, 0:PR] = (later[k] + acc * reach[k]).astype(BF16)
    r_copies = start([
        copy(ret.at[k], cr.at[core, y], r_sem, n, at(y_=k)) for n, k in enumerate(yy)
    ])
    waiting += r_copies
    cr[core, y] = ret[y]

    for n in range(2):
        wz[z, x, n : n + 1] = jnp.sum(tiles[n] + folded(acc * whole[n]), axis=0, keepdims=True)
    cross = sorted(
        ((p, q) for p in range(Z) for q in range(X) if p or q),
        key=lambda t: -min(t[0], Z - t[0]) - min(t[1], X - t[1]),
    )
    wz_copies = start([
        copy(wz.at[z, x], wz.at[z, x], wz_sem, n, at(z_=lax.rem(z + p, Z), x_=lax.rem(x + q, X)))
        for n, (p, q) in enumerate(cross)
    ])
    waiting += wz_copies
    arrive(wz_copies)
    sums = jnp.zeros((2, LANES), F32)
    for k in range(Z):
        for q in range(X):
            sums = sums + wz[k, q]
    wy[my_line] = sums
    wy_copies = start([
        copy(wy.at[my_line], wy.at[my_line], wy_sem, n, dev) for n, dev in enumerate(lines)
    ])
    waiting += wy_copies
    arrive(r_copies)
    cr_copies = start([copy(cr.at[core], cr.at[core], cr_sem, 0, at(c_=other))])
    waiting += cr_copies
    arrive(c_copies[1:2])
    arrive(cr_copies)
    for m_ in range(PIECES):
        r, c = rows_cols(m_)
        chip = cr[m_ % 2, m_ // 2].astype(F32)[0:PR]
        within = cx[m_ % 2, m_ // 2] + chip * (
            DECAY**2 * keep(block_cols(m_), chip_col2, chip_col1)
        )
        carry[r, c] = jnp.where(first, within, chip)

    prior_b = carry[...] * keep_12
    stores = []
    for f in (1, 0):
        moved = pltpu.roll(prior_b, lax.rem(WINDOW - (row0, row1)[f], WINDOW), 0)[0:BLOCK]
        prior = pltpu.roll(moved, (PUPIL - (col0, col1)[f]) & (PUPIL - 1), 1)
        out[f] = grad[f, 0:BLOCK] + prior
        stores.append(pltpu.make_async_copy(out.at[f], out_h.at[f], out_sem.at[f]))
        stores[-1].start()
        if f == 1:
            prior_b = (gb[1] + prior_b) * keep_01

    arrive(wy_copies)
    total = wy[0]
    for k in range(1, 2 * Y):
        total = total + wy[k]
    scale = -1.0 / (PUPIL * 2.0 * 2 * Y * Z)
    wind[0] = jnp.sum(total[0:1]) * scale
    wind[1] = jnp.sum(total[1:2]) * scale
    for n, k in enumerate(zz):
        pl.when(k < z)(zs_copies[n].wait_send)
    for store in stores:
        store.wait()
    for c in waiting:
        c.wait_send()


def on_device(Y, Z, X, phases, focal, shifts, mask):
    BLOCK = PUPIL // X
    WINDOW = BLOCK + HALO
    PIECES = 2 * Y
    PR = WINDOW * 4 // PIECES
    PR16 = -(-PR // 16) * 16
    by_pupil, by_focal = transform_tables()
    smem = pl.BlockSpec(memory_space=pltpu.SMEM)
    hbm = pl.BlockSpec(memory_space=pltpu.HBM)
    V = pltpu.VMEM

    def sems(n):
        return pltpu.SemaphoreType.DMA((2, n))

    scratch = [
        V((2, BLOCK, PUPIL), BF16),
        pltpu.SMEM((2, 2), jnp.int32),
        V((BLOCK, PUPIL), jnp.int32),
        V((PUPIL + HALO, PUPIL), BF16),
        V((PUPIL, PUPIL), BF16),
        V((4, BLOCK, 256), BF16),
        V((PUPIL, 256), BF16),
        V((2, FOCAL, LANES), BF16),
        V((HALO, PUPIL), BF16),
        V((HALO, PUPIL), BF16),
        V((2, PUPIL), F32),
        V((2, PUPIL), F32),
        V((Y, 2, 2, LANES), jnp.int32),
        V((Z, 2, LANES), jnp.int32),
        V((PUPIL, 256), BF16),
        V((X, WINDOW, 256), BF16),
        V((X, WINDOW, 256), BF16),
        V((2, WINDOW, PUPIL), F32),
        V((2, WINDOW, PUPIL), F32),
        V((2, Y, PR, LANES), F32),
        V((2, Y, PR, LANES), F32),
        V((Y, PR, LANES), F32),
        V((Y, PR, LANES), F32),
        V((Z, PR, LANES), F32),
        V((Y, PR16, LANES), BF16),
        V((2, Y, PR16, LANES), BF16),
        V((WINDOW, PUPIL), F32),
        V((2, WINDOW, PUPIL), F32),
        V((2, WINDOW, PUPIL), F32),
        V((2, Y, 2, PR, LANES), F32),
        V((Y, 2, PR, LANES), F32),
        V((Y, 2, PR, LANES), F32),
        V((Y, 2, PR, LANES), F32),
        V((Z, X, 2, LANES), F32),
        V((2 * Y, 2, LANES), F32),
        V((2, BLOCK, PUPIL), F32),
        pltpu.SemaphoreType.DMA((6,)),
        pltpu.SemaphoreType.DMA((2,)),
        sems(X), sems(X), sems(2), sems(2 * Y), sems(Z), sems(X), sems(2), sems(Y), sems(Z), sems(Y),
        sems(1), sems(1), sems(Y), sems(X * Z), sems(2 * Y), sems(1), pltpu.SemaphoreType.REGULAR,
    ]
    shapes = (
        jax.ShapeDtypeStruct((2, BLOCK, PUPIL), F32),
        jax.ShapeDtypeStruct((2,), F32),
    )
    return pl.pallas_call(
        functools.partial(body, Y, Z, X),
        name="adjoint_sweep",
        out_shape=shapes,
        in_specs=[hbm] * 6,
        out_specs=(hbm, smem),
        scratch_shapes=scratch,
        compiler_params=pltpu.CompilerParams(
            collective_id=1, has_side_effects=True, vmem_limit_bytes=63 << 20
        ),
    )(phases, focal, shifts, mask, jnp.asarray(by_pupil), jnp.asarray(by_focal))


def solution(mesh):
    X = mesh.shape["rows"]
    count = mesh.shape["tm"]
    Y = 8 if count == 128 else 2
    Z = count // (2 * Y)
    in_specs = (P("tm", "rows", None), P("tm", None, "rows", None), P("tm", None), P("rows", None))
    out_specs = (P("tm", "rows", None), P())
    return jax.shard_map(
        functools.partial(on_device, Y, Z, X), mesh=mesh, in_specs=in_specs, out_specs=out_specs,
        check_vma=False,
    )
```

```python
import functools
import math

import jax
import jax.numpy as jnp
import numpy as np
from jax import lax
from jax.experimental import pallas as pl
from jax.experimental.pallas import tpu as pltpu
from jax.sharding import PartitionSpec as P

PUPIL = 512
FOCAL = 256
HALO = 32
LANES = 128
DECAY = 0.999
MESH = pl.DeviceIdType.MESH
F32 = jnp.float32
BF16 = jnp.bfloat16


def transform_tables():
    focal_pos = np.arange(FOCAL, dtype=np.int32) - FOCAL // 2
    pupil_pos = np.arange(PUPIL, dtype=np.int32) - PUPIL // 2
    turns = np.mod(focal_pos[:, None] * pupil_pos[None, :], 2 * PUPIL)
    angle = turns.astype(np.float32) * np.float32(math.pi / PUPIL)
    factor = np.float32(1.0 / math.sqrt(PUPIL))
    cos_t = (np.cos(angle) * factor).astype(BF16)
    sin_t = (-np.sin(angle) * factor).astype(BF16)
    half = FOCAL // 2
    by_focal = np.concatenate([cos_t[:half], sin_t[:half], cos_t[half:], sin_t[half:]], axis=0)
    return np.ascontiguousarray(by_focal.T), by_focal


def body(
    Y, Z, X, phases_h, focal_h, shifts_h, mask_h, by_pupil_h, by_focal_h, out_h, wind,
    phases, shifts, mask, by_pupil, by_focal,
    y_send, y_recv, f_recv, h_send, h_recv, p_send, p_recv, s_recv, t_recv, resid, w_buf, w_recv,
    grad, gb, bseg, cx, ag, ys, zs, ret, cr, carry, wide_ph, d0b, qseg, qx, qc, qy, wz, wy, out,
    in_sem, out_sem, y_sem, f_sem, h_sem, s_sem, t_sem, w_sem, c_sem, ys_sem, zs_sem, r_sem, cr_sem,
    qx_sem, qy_sem, wz_sem, wy_sem, sc_sem, ring_sem,
):
    BLOCK = PUPIL // X
    WINDOW = BLOCK + HALO
    PIECES = 2 * Y
    PR = WINDOW * 4 // PIECES
    PR16 = -(-PR // 16) * 16
    me = lax.axis_index("tm")
    x = lax.axis_index("rows")
    core = lax.rem(me, 2)
    y = lax.rem(me // 2, Y)
    z = me // (2 * Y)
    other = 1 - core

    def at(x_=None, y_=None, z_=None, c_=None):
        zz = z if z_ is None else z_
        yy = y if y_ is None else y_
        cc = core if c_ is None else c_
        return ((zz * Y + yy) * 2 + cc, x if x_ is None else x_)

    def copy(src, dst, sems, n, device):
        return pltpu.make_async_remote_copy(
            src_ref=src, dst_ref=dst, send_sem=sems.at[0, n], recv_sem=sems.at[1, n],
            device_id=device, device_id_type=MESH,
        )

    def start(copies):
        for c in copies:
            c.start()
        return copies

    def arrive(copies):
        for c in copies:
            c.wait_recv()

    waiting = []

    def far_first(n):
        return sorted(range(1, n), key=lambda p: -min(p, n - p))

    xs = [lax.rem(x + p, X) for p in far_first(X)]
    yy = [lax.rem(y + p, Y) for p in far_first(Y)]
    zz = [lax.rem(z + p, Z) for p in far_first(Z)]
    lines = [
        at(y_=lax.rem(y + p, Y), c_=lax.rem(core + q, 2))
        for p in far_first(Y) for q in range(2)
    ] + [at(c_=other)]

    zs[...] = jnp.zeros((Z, PR, LANES), F32)
    def ring(d):
        near_y = [at(y_=lax.rem(y + p, Y)) for p in sorted({d % Y, -d % Y} - {0})]
        return near_y + [at(z_=lax.rem(z + p, Z)) for p in sorted({d % Z, -d % Z} - {0})]

    relayed = max(Y, Z) > 5

    barrier = pltpu.get_barrier_semaphore()
    entry = [at(x_=k) for k in xs] + ring(2) + ring(1) + [at(c_=other)]
    for dev in entry:
        pl.semaphore_signal(barrier, inc=1, device_id=dev, device_id_type=MESH)
    q_rows = FOCAL // X
    q_of = lambda k: pl.ds(pl.multiple_of(k * q_rows, q_rows), q_rows)
    cols_of = lambda k: pl.ds(pl.multiple_of(lax.rem(k, 2) * LANES, LANES), LANES)
    loads = [
        pltpu.make_async_copy(src, dst, in_sem.at[n])
        for n, (src, dst) in enumerate([
            (shifts_h, shifts),
            (phases_h, phases),
            (mask_h, mask),
            (by_pupil_h, by_pupil.at[0:PUPIL]),
            (by_focal_h, by_focal),
            (focal_h.at[x // 2, :, :, cols_of(x)], f_recv.at[:, q_of(x), :]),
        ])
    ]
    for load in loads:
        load.start()

    for load in loads[0:3]:
        load.wait()
    a0, b0, a1, b1 = shifts[0, 0], shifts[0, 1], shifts[1, 0], shifts[1, 1]
    live = jnp.where(mask[...] == 1, 1.0, 0.0).astype(F32)
    h_send[0:HALO] = live[0:HALO].astype(BF16)
    for f in range(2):
        p_send[f : f + 1] = phases[f, 0:16].astype(F32)[0:1]
    my_line = y * 2 + core
    s_recv[y, core, 0:1] = jnp.full((1, LANES), a0 + a1, jnp.int32)
    s_recv[y, core, 1:2] = jnp.full((1, LANES), b0 + b1, jnp.int32)
    pl.semaphore_wait(barrier, len(entry))
    if relayed:
        for dev in ring(2):
            pl.semaphore_signal(ring_sem, inc=1, device_id=dev, device_id_type=MESH)
    sc_copies = start([copy(s_recv.at[y, core], s_recv.at[y, core], sc_sem, 0, at(c_=other))])
    waiting += sc_copies
    loads[3].wait()
    for f in range(2):
        masked = (phases[f].astype(F32) * live).astype(BF16)
        yv = jnp.dot(masked, by_pupil[0:PUPIL], preferred_element_type=F32).astype(BF16)
        y_send[2 * f] = yv[:, 0:256]
        y_send[2 * f + 1] = yv[:, 256:512]


    rows_of = lambda k: pl.ds(pl.multiple_of(k * BLOCK, BLOCK), BLOCK)
    y_copies = start([
        copy(y_send.at[k], y_recv.at[rows_of(x)], y_sem, n, at(x_=k)) for n, k in enumerate(xs)
    ])
    f_copies = start([
        copy(focal_h.at[k // 2, :, :, cols_of(k)], f_recv.at[:, q_of(x), :], f_sem, n, at(x_=k))
        for n, k in enumerate(xs)
    ])
    waiting += y_copies + f_copies
    if relayed:
        pl.semaphore_wait(ring_sem, len(ring(2)))
    arrive(sc_copies)
    s_copies = start([
        copy(s_recv.at[y], s_recv.at[y], s_sem, n, at(y_=k)) for n, k in enumerate(yy)
    ])
    waiting += s_copies

    y_recv[rows_of(x)] = y_send[x]
    by_pupil[PUPIL : PUPIL + HALO] = jnp.zeros((HALO, PUPIL), BF16)
    if PR16 > PR:
        ret[:, PR:PR16] = jnp.zeros((Y, PR16 - PR, LANES), BF16)

    arrive(y_copies)
    above = at(x_=lax.rem(x + X - 1, X))
    h_copies = start([
        copy(p_send, p_recv, h_sem, 0, above), copy(h_send, h_recv, h_sem, 1, above)
    ])
    waiting += h_copies
    loads[4].wait()
    m = jnp.dot(by_focal[...], y_recv[...], preferred_element_type=F32)
    loads[5].wait()
    arrive(f_copies)
    for h in range(2):
        mc, ms = m[256 * h : 256 * h + 128], m[256 * h + 128 : 256 * h + 256]
        e_real = mc[:, 0:128] - ms[:, 128:256]
        e_imag = mc[:, 128:256] + ms[:, 0:128]
        r_real = (f_recv[0, 128 * h : 128 * h + 128].astype(F32) - e_real).astype(BF16)
        r_imag = (f_recv[1, 128 * h : 128 * h + 128].astype(F32) - e_imag).astype(BF16)
        resid[256 * h : 256 * h + 128, 0:128] = r_real
        resid[256 * h : 256 * h + 128, 128:256] = r_imag
        resid[256 * h + 128 : 256 * h + 256, 0:128] = r_imag
        resid[256 * h + 128 : 256 * h + 256, 128:256] = -r_real
    win_of = lambda k: pl.ds(pl.multiple_of(k * BLOCK, BLOCK), WINDOW)
    w_copies = []
    for n, k in enumerate(xs + [x]):
        rows = jnp.dot(by_pupil[win_of(k)], resid[...], preferred_element_type=F32)
        if n == X - 1:
            w_recv[x] = rows.astype(BF16)
        else:
            w_buf[n] = rows.astype(BF16)
            w_copies += start([copy(w_buf.at[n], w_recv.at[x], w_sem, n, at(x_=k))])
    waiting += w_copies

    arrive(s_copies)
    total_shift = jnp.zeros((2, LANES), jnp.int32)
    for k in range(Y):
        for c in range(2):
            total_shift = total_shift + s_recv[k, c]
    t_recv[z] = total_shift
    t_copies = start([
        copy(t_recv.at[z], t_recv.at[z], t_sem, n, at(z_=k)) for n, k in enumerate(zz)
    ])
    waiting += t_copies

    lane = lax.broadcasted_iota(jnp.int32, (1, LANES), 1)
    wide = lax.broadcasted_iota(jnp.int32, (1, PUPIL), 1)

    arrive(h_copies)
    inner = jnp.where(x < X - 1, 1.0, 0.0).astype(F32)
    for f in range(2):
        wide_ph[f, 0:BLOCK] = phases[f].astype(F32)
        wide_ph[f, BLOCK:WINDOW] = jnp.zeros((HALO, PUPIL), F32)
        wide_ph[f, BLOCK : BLOCK + 1] = p_recv[f : f + 1] * inner
    arrive(w_copies)
    for f in range(2):
        g = jnp.dot(w_recv[2 * f], by_focal[0:256], preferred_element_type=F32) + jnp.dot(
            w_recv[2 * f + 1], by_focal[256:512], preferred_element_type=F32
        )
        grad[f, 0:BLOCK] = g[0:BLOCK] * live
        grad[f, BLOCK:WINDOW] = g[BLOCK:WINDOW] * h_recv[0:HALO].astype(F32)
    arrive(t_copies)
    zero_tile = jnp.zeros((2, LANES), jnp.int32)
    beyond = zero_tile
    z_cols = [None] * Z + [zero_tile[1:2]]
    for k in reversed(range(Z)):
        beyond = beyond + jnp.where(k > z, t_recv[k], zero_tile)
        z_cols[k] = z_cols[k + 1] + t_recv[k, 1:2]
    chip_end = beyond[1:2]
    y_cols = [None] * Y + [chip_end]
    own_sum, c0_sum, c1_sum, c2_sum = beyond, beyond, beyond, beyond
    for k in reversed(range(Y)):
        y_cols[k] = y_cols[k + 1] + s_recv[k, 1, 1:2] + s_recv[k, 0, 1:2]
        for c in range(2):
            line = 2 * k + c
            tile = s_recv[k, c]
            own_sum = own_sum + jnp.where(line >= my_line, tile, zero_tile)
            c0_sum = c0_sum + jnp.where(line >= 2 * y, tile, zero_tile)
            c1_sum = c1_sum + jnp.where(line >= 2 * y + 1, tile, zero_tile)
            c2_sum = c2_sum + jnp.where(line >= 2 * y + 2, tile, zero_tile)
    row0 = jnp.max(own_sum[0:1])
    row1 = row0 - a0
    col0 = jnp.max(own_sum[1:2])
    col1 = col0 - b0
    col2 = col1 - b1
    chip_col0, chip_col1, chip_col2 = c0_sum[1:2], c1_sum[1:2], c2_sum[1:2]

    def keep(cols, late, early):
        return jnp.where(((cols - late) & (PUPIL - 1)) >= early - late, 1.0, 0.0).astype(F32)

    def block_cols(piece):
        return lax.rem(piece, 4) * LANES + lane

    def rows_cols(piece):
        r, c = piece // 4, piece % 4
        return slice(PR * r, PR * r + PR), slice(LANES * c, LANES * c + LANES)

    def shifted(value, f):
        turned = pltpu.roll(value, (row0, row1)[f], 0)
        return pltpu.roll(turned, (col0, col1)[f] & (PUPIL - 1), 1)

    def folded(value):
        parts = jnp.sum(value.reshape(value.shape[0] // 8, 8, value.shape[1]), axis=0)
        total = parts[:, 0:LANES]
        for c in range(1, value.shape[1] // LANES):
            total = total + parts[:, LANES * c : LANES * c + LANES]
        return total

    keep_01 = DECAY * keep(wide, col1, col0)
    keep_12 = DECAY * keep(wide, col2, col1)
    for f in range(2):
        gb[f] = shifted(grad[f], f)
    seg = gb[0] + gb[1] * keep_01

    for m_ in range(PIECES):
        r, c = rows_cols(m_)
        bseg[m_ % 2, m_ // 2] = seg[r, c]

    c_copies = start([copy(bseg.at[other], cx.at[other], c_sem, 0, at(c_=other))])
    waiting += c_copies
    row_at = lax.broadcasted_iota(jnp.int32, (WINDOW, 1), 0)
    steps = []
    for f in range(2):
        placed = shifted(wide_ph[f], f)
        row = row_at - (row0, row1)[f]
        inside = jnp.where((row >= 0) & (row < BLOCK), 1.0, 0.0).astype(F32)
        last = wide == ((PUPIL - 1 + (col0, col1)[f]) & (PUPIL - 1))
        down = (pltpu.roll(placed, WINDOW - 1, 0) - placed) * inside
        side = (jnp.where(last, 0.0, pltpu.roll(placed, PUPIL - 1, 1)) - placed) * inside
        steps.append((down, side))
    for n in range(2):
        d0b[n] = keep_01 * steps[0][n]
        weight = keep_12 * (steps[1][n] + d0b[n])
        for m_ in range(PIECES):
            r, c = rows_cols(m_)
            qseg[m_ % 2, m_ // 2, n] = weight[r, c]
    qx_copies = start([copy(qseg.at[other], qx, qx_sem, 0, at(c_=other))])
    waiting += qx_copies
    arrive(c_copies)
    first = core == 0
    for k in range(Y):
        mine, theirs = bseg[core, k], cx[core, k]
        early = jnp.where(first, mine, theirs)
        late = jnp.where(first, theirs, mine)
        ag[k] = early + late * (DECAY**2 * keep(block_cols(2 * k + core), chip_col1, chip_col0))
    ys_copies = start([
        copy(ag.at[k], ys.at[y], ys_sem, n, at(y_=k)) for n, k in enumerate(yy)
    ])
    waiting += ys_copies
    ys[y] = ag[y]
    arrive(qx_copies)
    tiles = [folded(gb[1] * d0b[n]) for n in range(2)]
    for k in range(Y):
        late = jnp.where(first, cx[core, k], bseg[core, k])
        keep_k = DECAY**2 * keep(block_cols(2 * k + core), chip_col2, chip_col1)
        for n in range(2):
            mine, theirs = qseg[core, k, n], qx[k, n]
            early_q = jnp.where(first, mine, theirs)
            late_q = jnp.where(first, theirs, mine)
            tiles[n] = tiles[n] + folded(late * early_q)
            qc[k, n] = late_q + keep_k * early_q
    qy_copies = start([
        copy(qc.at[k], qy.at[y], qy_sem, n, at(y_=k)) for n, k in enumerate(yy)
    ])
    waiting += qy_copies
    qy[y] = qc[y]
    rest_copies = start([copy(bseg.at[core], cx.at[core], c_sem, 1, at(c_=other))])
    waiting += rest_copies
    arrive(ys_copies)
    my_cols = block_cols(my_line)
    later = [None] * Y
    later[Y - 1] = jnp.zeros((PR, LANES), F32)
    for k in reversed(range(Y - 1)):
        later[k] = ys[k + 1] + later[k + 1] * (DECAY**4 * keep(my_cols, y_cols[k + 2], y_cols[k + 1]))
    zs[z] = ys[0] + later[0] * (DECAY**4 * keep(my_cols, y_cols[1], y_cols[0]))
    zs_copies = [copy(zs.at[z], zs.at[z], zs_sem, n, at(z_=k)) for n, k in enumerate(zz)]
    for n, k in enumerate(zz):
        pl.when(k < z)(zs_copies[n].start)
    reach = [
        DECAY ** (4 * (Y - 1 - k)) * keep(my_cols, chip_end, y_cols[k + 1]) for k in range(Y)
    ]
    arrive(qy_copies)
    whole = [jnp.zeros((PR, LANES), F32) for _ in range(2)]
    for k in range(Y):
        for n in range(2):
            tiles[n] = tiles[n] + folded(later[k] * qy[k, n])
            whole[n] = whole[n] + reach[k] * qy[k, n]
    for n, p in enumerate(far_first(Z)):
        pl.when(lax.rem(z + Z - p, Z) > z)(zs_copies[n].wait_recv)
    acc = jnp.zeros((PR, LANES), F32)
    for k in reversed(range(1, Z)):
        new = zs[k] + acc * (DECAY ** (4 * Y) * keep(my_cols, z_cols[k + 1], z_cols[k]))
        acc = jnp.where(k > z, new, acc)
    for k in range(Y):
        ret[k, 0:PR] = (later[k] + acc * reach[k]).astype(BF16)
    r_copies = start([
        copy(ret.at[k], cr.at[core, y], r_sem, n, at(y_=k)) for n, k in enumerate(yy)
    ])
    waiting += r_copies
    cr[core, y] = ret[y]

    for n in range(2):
        wz[z, x, n : n + 1] = jnp.sum(tiles[n] + folded(acc * whole[n]), axis=0, keepdims=True)
    cross = sorted(
        ((p, q) for p in range(Z) for q in range(X) if p or q),
        key=lambda t: -min(t[0], Z - t[0]) - min(t[1], X - t[1]),
    )
    wz_copies = start([
        copy(wz.at[z, x], wz.at[z, x], wz_sem, n, at(z_=lax.rem(z + p, Z), x_=lax.rem(x + q, X)))
        for n, (p, q) in enumerate(cross)
    ])
    waiting += wz_copies
    arrive(wz_copies)
    sums = jnp.zeros((2, LANES), F32)
    for k in range(Z):
        for q in range(X):
            sums = sums + wz[k, q]
    wy[my_line] = sums
    wy_copies = start([
        copy(wy.at[my_line], wy.at[my_line], wy_sem, n, dev) for n, dev in enumerate(lines)
    ])
    waiting += wy_copies
    arrive(r_copies)
    cr_copies = start([copy(cr.at[core], cr.at[core], cr_sem, 0, at(c_=other))])
    waiting += cr_copies
    arrive(rest_copies)
    arrive(cr_copies)
    for m_ in range(PIECES):
        r, c = rows_cols(m_)
        chip = cr[m_ % 2, m_ // 2].astype(F32)[0:PR]
        within = cx[m_ % 2, m_ // 2] + chip * (
            DECAY**2 * keep(block_cols(m_), chip_col2, chip_col1)
        )
        carry[r, c] = jnp.where(first, within, chip)

    prior_b = carry[...] * keep_12
    stores = []
    for f in (1, 0):
        moved = pltpu.roll(prior_b, lax.rem(WINDOW - (row0, row1)[f], WINDOW), 0)[0:BLOCK]
        prior = pltpu.roll(moved, (PUPIL - (col0, col1)[f]) & (PUPIL - 1), 1)
        out[f] = grad[f, 0:BLOCK] + prior
        stores.append(pltpu.make_async_copy(out.at[f], out_h.at[f], out_sem.at[f]))
        stores[-1].start()
        if f == 1:
            prior_b = (gb[1] + prior_b) * keep_01

    arrive(wy_copies)
    total = wy[0]
    for k in range(1, 2 * Y):
        total = total + wy[k]
    scale = -1.0 / (PUPIL * 2.0 * 2 * Y * Z)
    wind[0] = jnp.sum(total[0:1]) * scale
    wind[1] = jnp.sum(total[1:2]) * scale
    for n, k in enumerate(zz):
        pl.when(k < z)(zs_copies[n].wait_send)
    for store in stores:
        store.wait()
    for c in waiting:
        c.wait_send()


def on_device(Y, Z, X, phases, focal, shifts, mask):
    BLOCK = PUPIL // X
    WINDOW = BLOCK + HALO
    PIECES = 2 * Y
    PR = WINDOW * 4 // PIECES
    PR16 = -(-PR // 16) * 16
    by_pupil, by_focal = transform_tables()
    smem = pl.BlockSpec(memory_space=pltpu.SMEM)
    hbm = pl.BlockSpec(memory_space=pltpu.HBM)
    V = pltpu.VMEM

    def sems(n):
        return pltpu.SemaphoreType.DMA((2, n))

    scratch = [
        V((2, BLOCK, PUPIL), BF16),
        pltpu.SMEM((2, 2), jnp.int32),
        V((BLOCK, PUPIL), jnp.int32),
        V((PUPIL + HALO, PUPIL), BF16),
        V((PUPIL, PUPIL), BF16),
        V((4, BLOCK, 256), BF16),
        V((PUPIL, 256), BF16),
        V((2, FOCAL, LANES), BF16),
        V((HALO, PUPIL), BF16),
        V((HALO, PUPIL), BF16),
        V((2, PUPIL), F32),
        V((2, PUPIL), F32),
        V((Y, 2, 2, LANES), jnp.int32),
        V((Z, 2, LANES), jnp.int32),
        V((PUPIL, 256), BF16),
        V((X, WINDOW, 256), BF16),
        V((X, WINDOW, 256), BF16),
        V((2, WINDOW, PUPIL), F32),
        V((2, WINDOW, PUPIL), F32),
        V((2, Y, PR, LANES), F32),
        V((2, Y, PR, LANES), F32),
        V((Y, PR, LANES), F32),
        V((Y, PR, LANES), F32),
        V((Z, PR, LANES), F32),
        V((Y, PR16, LANES), BF16),
        V((2, Y, PR16, LANES), BF16),
        V((WINDOW, PUPIL), F32),
        V((2, WINDOW, PUPIL), F32),
        V((2, WINDOW, PUPIL), F32),
        V((2, Y, 2, PR, LANES), F32),
        V((Y, 2, PR, LANES), F32),
        V((Y, 2, PR, LANES), F32),
        V((Y, 2, PR, LANES), F32),
        V((Z, X, 2, LANES), F32),
        V((2 * Y, 2, LANES), F32),
        V((2, BLOCK, PUPIL), F32),
        pltpu.SemaphoreType.DMA((6,)),
        pltpu.SemaphoreType.DMA((2,)),
        sems(X), sems(X), sems(2), sems(2 * Y), sems(Z), sems(X), sems(2), sems(Y), sems(Z), sems(Y),
        sems(1), sems(1), sems(Y), sems(X * Z), sems(2 * Y), sems(1), pltpu.SemaphoreType.REGULAR,
    ]
    shapes = (
        jax.ShapeDtypeStruct((2, BLOCK, PUPIL), F32),
        jax.ShapeDtypeStruct((2,), F32),
    )
    return pl.pallas_call(
        functools.partial(body, Y, Z, X),
        name="adjoint_sweep",
        out_shape=shapes,
        in_specs=[hbm] * 6,
        out_specs=(hbm, smem),
        scratch_shapes=scratch,
        compiler_params=pltpu.CompilerParams(
            collective_id=1, has_side_effects=True, vmem_limit_bytes=63 << 20
        ),
    )(phases, focal, shifts, mask, jnp.asarray(by_pupil), jnp.asarray(by_focal))


def solution(mesh):
    X = mesh.shape["rows"]
    count = mesh.shape["tm"]
    Y = 8 if count == 128 else 2
    Z = count // (2 * Y)
    in_specs = (P("tm", "rows", None), P("tm", None, "rows", None), P("tm", None), P("rows", None))
    out_specs = (P("tm", "rows", None), P())
    return jax.shard_map(
        functools.partial(on_device, Y, Z, X), mesh=mesh, in_specs=in_specs, out_specs=out_specs,
        check_vma=False,
    )
```

```python
import functools
import math

import jax
import jax.numpy as jnp
import numpy as np
from jax import lax
from jax.experimental import pallas as pl
from jax.experimental.pallas import tpu as pltpu
from jax.sharding import PartitionSpec as P

PUPIL = 512
FOCAL = 256
HALO = 32
LANES = 128
DECAY = 0.999
MESH = pl.DeviceIdType.MESH
F32 = jnp.float32
BF16 = jnp.bfloat16


def transform_tables():
    focal_pos = np.arange(FOCAL, dtype=np.int32) - FOCAL // 2
    pupil_pos = np.arange(PUPIL, dtype=np.int32) - PUPIL // 2
    turns = np.mod(focal_pos[:, None] * pupil_pos[None, :], 2 * PUPIL)
    angle = turns.astype(np.float32) * np.float32(math.pi / PUPIL)
    factor = np.float32(1.0 / math.sqrt(PUPIL))
    cos_t = (np.cos(angle) * factor).astype(BF16)
    sin_t = (-np.sin(angle) * factor).astype(BF16)
    half = FOCAL // 2
    by_focal = np.concatenate([cos_t[:half], sin_t[:half], cos_t[half:], sin_t[half:]], axis=0)
    return np.ascontiguousarray(by_focal.T), by_focal


def body(
    Y, Z, X, phases_h, focal_h, shifts_h, mask_h, by_pupil_h, by_focal_h, out_h, wind,
    phases, shifts, mask, by_pupil, by_focal,
    y_send, y_recv, f_recv, h_send, h_recv, p_send, p_recv, s_recv, t_recv, resid, w_buf, w_recv,
    grad, gb, bseg, cx, ag, ys, zs, ret, cr, carry, wide_ph, d0b, qseg, qx, qc, qy, wz, wy, out,
    in_sem, out_sem, y_sem, f_sem, h_sem, s_sem, t_sem, w_sem, c_sem, ys_sem, zs_sem, r_sem, cr_sem,
    qx_sem, qy_sem, wz_sem, wy_sem, sc_sem, ring_sem,
):
    BLOCK = PUPIL // X
    WINDOW = BLOCK + HALO
    PIECES = 2 * Y
    PR = WINDOW * 4 // PIECES
    PR16 = -(-PR // 16) * 16
    me = lax.axis_index("tm")
    x = lax.axis_index("rows")
    core = lax.rem(me, 2)
    y = lax.rem(me // 2, Y)
    z = me // (2 * Y)
    other = 1 - core

    def at(x_=None, y_=None, z_=None, c_=None):
        zz = z if z_ is None else z_
        yy = y if y_ is None else y_
        cc = core if c_ is None else c_
        return ((zz * Y + yy) * 2 + cc, x if x_ is None else x_)

    def copy(src, dst, sems, n, device):
        return pltpu.make_async_remote_copy(
            src_ref=src, dst_ref=dst, send_sem=sems.at[0, n], recv_sem=sems.at[1, n],
            device_id=device, device_id_type=MESH,
        )

    def start(copies):
        for c in copies:
            c.start()
        return copies

    def arrive(copies):
        for c in copies:
            c.wait_recv()

    waiting = []

    def far_first(n):
        return sorted(range(1, n), key=lambda p: -min(p, n - p))

    xs = [lax.rem(x + p, X) for p in far_first(X)]
    yy = [lax.rem(y + p, Y) for p in far_first(Y)]
    zz = [lax.rem(z + p, Z) for p in far_first(Z)]
    lines = [
        at(y_=lax.rem(y + p, Y), c_=lax.rem(core + q, 2))
        for p in far_first(Y) for q in range(2)
    ] + [at(c_=other)]

    zs[...] = jnp.zeros((Z, PR, LANES), F32)
    def ring(d):
        near_y = [at(y_=lax.rem(y + p, Y)) for p in sorted({d % Y, -d % Y} - {0})]
        return near_y + [at(z_=lax.rem(z + p, Z)) for p in sorted({d % Z, -d % Z} - {0})]

    relayed = max(Y, Z) > 5

    barrier = pltpu.get_barrier_semaphore()
    entry = [at(x_=k) for k in xs] + ring(2) + ring(1) + [at(c_=other)]
    for dev in entry:
        pl.semaphore_signal(barrier, inc=1, device_id=dev, device_id_type=MESH)
    q_rows = FOCAL // X
    q_of = lambda k: pl.ds(pl.multiple_of(k * q_rows, q_rows), q_rows)
    cols_of = lambda k: pl.ds(pl.multiple_of(lax.rem(k, 2) * LANES, LANES), LANES)
    loads = [
        pltpu.make_async_copy(src, dst, in_sem.at[n])
        for n, (src, dst) in enumerate([
            (shifts_h, shifts),
            (phases_h, phases),
            (mask_h, mask),
            (by_pupil_h, by_pupil.at[0:PUPIL]),
            (by_focal_h, by_focal),
            (focal_h.at[x // 2, :, :, cols_of(x)], f_recv.at[:, q_of(x), :]),
        ])
    ]
    for load in loads:
        load.start()

    for load in loads[0:3]:
        load.wait()
    a0, b0, a1, b1 = shifts[0, 0], shifts[0, 1], shifts[1, 0], shifts[1, 1]
    live = jnp.where(mask[...] == 1, 1.0, 0.0).astype(F32)
    h_send[0:HALO] = live[0:HALO].astype(BF16)
    for f in range(2):
        p_send[f : f + 1] = phases[f, 0:16].astype(F32)[0:1]
    my_line = y * 2 + core
    s_recv[y, core, 0:1] = jnp.full((1, LANES), a0 + a1, jnp.int32)
    s_recv[y, core, 1:2] = jnp.full((1, LANES), b0 + b1, jnp.int32)
    pl.semaphore_wait(barrier, len(entry))
    if relayed:
        for dev in ring(2):
            pl.semaphore_signal(ring_sem, inc=1, device_id=dev, device_id_type=MESH)
    sc_copies = start([copy(s_recv.at[y, core], s_recv.at[y, core], sc_sem, 0, at(c_=other))])
    waiting += sc_copies
    loads[3].wait()
    for f in range(2):
        masked = (phases[f].astype(F32) * live).astype(BF16)
        yv = jnp.dot(masked, by_pupil[0:PUPIL], preferred_element_type=F32).astype(BF16)
        y_send[2 * f] = yv[:, 0:256]
        y_send[2 * f + 1] = yv[:, 256:512]


    rows_of = lambda k: pl.ds(pl.multiple_of(k * BLOCK, BLOCK), BLOCK)
    y_copies = start([
        copy(y_send.at[k], y_recv.at[rows_of(x)], y_sem, n, at(x_=k)) for n, k in enumerate(xs)
    ])
    f_copies = start([
        copy(focal_h.at[k // 2, :, :, cols_of(k)], f_recv.at[:, q_of(x), :], f_sem, n, at(x_=k))
        for n, k in enumerate(xs)
    ])
    waiting += y_copies + f_copies
    if relayed:
        pl.semaphore_wait(ring_sem, len(ring(2)))
    arrive(sc_copies)
    s_copies = start([
        copy(s_recv.at[y], s_recv.at[y], s_sem, n, at(y_=k)) for n, k in enumerate(yy)
    ])
    waiting += s_copies

    y_recv[rows_of(x)] = y_send[x]
    by_pupil[PUPIL : PUPIL + HALO] = jnp.zeros((HALO, PUPIL), BF16)
    if PR16 > PR:
        ret[:, PR:PR16] = jnp.zeros((Y, PR16 - PR, LANES), BF16)

    arrive(y_copies)
    above = at(x_=lax.rem(x + X - 1, X))
    h_copies = start([
        copy(p_send, p_recv, h_sem, 0, above), copy(h_send, h_recv, h_sem, 1, above)
    ])
    waiting += h_copies
    loads[4].wait()
    m = jnp.dot(by_focal[...], y_recv[...], preferred_element_type=F32)
    loads[5].wait()
    arrive(f_copies)
    for h in range(2):
        mc, ms = m[256 * h : 256 * h + 128], m[256 * h + 128 : 256 * h + 256]
        e_real = mc[:, 0:128] - ms[:, 128:256]
        e_imag = mc[:, 128:256] + ms[:, 0:128]
        r_real = (f_recv[0, 128 * h : 128 * h + 128].astype(F32) - e_real).astype(BF16)
        r_imag = (f_recv[1, 128 * h : 128 * h + 128].astype(F32) - e_imag).astype(BF16)
        resid[256 * h : 256 * h + 128, 0:128] = r_real
        resid[256 * h : 256 * h + 128, 128:256] = r_imag
        resid[256 * h + 128 : 256 * h + 256, 0:128] = r_imag
        resid[256 * h + 128 : 256 * h + 256, 128:256] = -r_real
    win_of = lambda k: pl.ds(pl.multiple_of(k * BLOCK, BLOCK), WINDOW)
    w_copies = []
    for n, k in enumerate(xs + [x]):
        rows = jnp.dot(by_pupil[win_of(k)], resid[...], preferred_element_type=F32)
        if n == X - 1:
            w_recv[x] = rows.astype(BF16)
        else:
            w_buf[n] = rows.astype(BF16)
            w_copies += start([copy(w_buf.at[n], w_recv.at[x], w_sem, n, at(x_=k))])
    waiting += w_copies

    arrive(s_copies)
    total_shift = jnp.zeros((2, LANES), jnp.int32)
    for k in range(Y):
        for c in range(2):
            total_shift = total_shift + s_recv[k, c]
    t_recv[z] = total_shift
    t_copies = start([
        copy(t_recv.at[z], t_recv.at[z], t_sem, n, at(z_=k)) for n, k in enumerate(zz)
    ])
    waiting += t_copies

    lane = lax.broadcasted_iota(jnp.int32, (1, LANES), 1)
    wide = lax.broadcasted_iota(jnp.int32, (1, PUPIL), 1)

    arrive(h_copies)
    inner = jnp.where(x < X - 1, 1.0, 0.0).astype(F32)
    for f in range(2):
        wide_ph[f, 0:BLOCK] = phases[f].astype(F32)
        wide_ph[f, BLOCK:WINDOW] = jnp.zeros((HALO, PUPIL), F32)
        wide_ph[f, BLOCK : BLOCK + 1] = p_recv[f : f + 1] * inner
    arrive(w_copies)
    for f in range(2):
        g = jnp.dot(w_recv[2 * f], by_focal[0:256], preferred_element_type=F32) + jnp.dot(
            w_recv[2 * f + 1], by_focal[256:512], preferred_element_type=F32
        )
        grad[f, 0:BLOCK] = g[0:BLOCK] * live
        grad[f, BLOCK:WINDOW] = g[BLOCK:WINDOW] * h_recv[0:HALO].astype(F32)
    arrive(t_copies)
    zero_tile = jnp.zeros((2, LANES), jnp.int32)
    beyond = zero_tile
    z_cols = [None] * Z + [zero_tile[1:2]]
    for k in reversed(range(Z)):
        beyond = beyond + jnp.where(k > z, t_recv[k], zero_tile)
        z_cols[k] = z_cols[k + 1] + t_recv[k, 1:2]
    chip_end = beyond[1:2]
    y_cols = [None] * Y + [chip_end]
    own_sum, c0_sum, c1_sum, c2_sum = beyond, beyond, beyond, beyond
    for k in reversed(range(Y)):
        y_cols[k] = y_cols[k + 1] + s_recv[k, 1, 1:2] + s_recv[k, 0, 1:2]
        for c in range(2):
            line = 2 * k + c
            tile = s_recv[k, c]
            own_sum = own_sum + jnp.where(line >= my_line, tile, zero_tile)
            c0_sum = c0_sum + jnp.where(line >= 2 * y, tile, zero_tile)
            c1_sum = c1_sum + jnp.where(line >= 2 * y + 1, tile, zero_tile)
            c2_sum = c2_sum + jnp.where(line >= 2 * y + 2, tile, zero_tile)
    row0 = jnp.max(own_sum[0:1])
    row1 = row0 - a0
    col0 = jnp.max(own_sum[1:2])
    col1 = col0 - b0
    col2 = col1 - b1
    chip_col0, chip_col1, chip_col2 = c0_sum[1:2], c1_sum[1:2], c2_sum[1:2]

    def keep(cols, late, early):
        return jnp.where(((cols - late) & (PUPIL - 1)) >= early - late, 1.0, 0.0).astype(F32)

    def block_cols(piece):
        return lax.rem(piece, 4) * LANES + lane

    def rows_cols(piece):
        r, c = piece // 4, piece % 4
        return slice(PR * r, PR * r + PR), slice(LANES * c, LANES * c + LANES)

    def shifted(value, f):
        turned = pltpu.roll(value, (row0, row1)[f], 0)
        return pltpu.roll(turned, (col0, col1)[f] & (PUPIL - 1), 1)

    def folded(value):
        parts = jnp.sum(value.reshape(value.shape[0] // 8, 8, value.shape[1]), axis=0)
        total = parts[:, 0:LANES]
        for c in range(1, value.shape[1] // LANES):
            total = total + parts[:, LANES * c : LANES * c + LANES]
        return total

    keep_01 = DECAY * keep(wide, col1, col0)
    keep_12 = DECAY * keep(wide, col2, col1)
    for f in range(2):
        gb[f] = shifted(grad[f], f)
    seg = gb[0] + gb[1] * keep_01

    for m_ in range(PIECES):
        r, c = rows_cols(m_)
        bseg[m_ % 2, m_ // 2] = seg[r, c]

    c_copies = start([copy(bseg.at[other], cx.at[other], c_sem, 0, at(c_=other))])
    waiting += c_copies
    row_at = lax.broadcasted_iota(jnp.int32, (WINDOW, 1), 0)
    steps = []
    for f in range(2):
        placed = shifted(wide_ph[f], f)
        row = row_at - (row0, row1)[f]
        inside = jnp.where((row >= 0) & (row < BLOCK), 1.0, 0.0).astype(F32)
        last = wide == ((PUPIL - 1 + (col0, col1)[f]) & (PUPIL - 1))
        down = (pltpu.roll(placed, WINDOW - 1, 0) - placed) * inside
        side = (jnp.where(last, 0.0, pltpu.roll(placed, PUPIL - 1, 1)) - placed) * inside
        steps.append((down, side))
    for n in range(2):
        d0b[n] = keep_01 * steps[0][n]
        weight = keep_12 * (steps[1][n] + d0b[n])
        for m_ in range(PIECES):
            r, c = rows_cols(m_)
            qseg[m_ % 2, m_ // 2, n] = weight[r, c]
    qx_copies = start([copy(qseg.at[other], qx, qx_sem, 0, at(c_=other))])
    waiting += qx_copies
    arrive(c_copies)
    first = core == 0
    for k in range(Y):
        mine, theirs = bseg[core, k], cx[core, k]
        early = jnp.where(first, mine, theirs)
        late = jnp.where(first, theirs, mine)
        ag[k] = early + late * (DECAY**2 * keep(block_cols(2 * k + core), chip_col1, chip_col0))
    ys_copies = start([
        copy(ag.at[k], ys.at[y], ys_sem, n, at(y_=k)) for n, k in enumerate(yy)
    ])
    waiting += ys_copies
    ys[y] = ag[y]
    arrive(qx_copies)
    tiles = [folded(gb[1] * d0b[n]) for n in range(2)]
    for k in range(Y):
        late = jnp.where(first, cx[core, k], bseg[core, k])
        keep_k = DECAY**2 * keep(block_cols(2 * k + core), chip_col2, chip_col1)
        for n in range(2):
            mine, theirs = qseg[core, k, n], qx[k, n]
            early_q = jnp.where(first, mine, theirs)
            late_q = jnp.where(first, theirs, mine)
            tiles[n] = tiles[n] + folded(late * early_q)
            qc[k, n] = late_q + keep_k * early_q
    qy_copies = start([
        copy(qc.at[k], qy.at[y], qy_sem, n, at(y_=k)) for n, k in enumerate(yy)
    ])
    waiting += qy_copies
    qy[y] = qc[y]
    rest_copies = start([copy(bseg.at[core], cx.at[core], c_sem, 1, at(c_=other))])
    waiting += rest_copies
    arrive(ys_copies)
    my_cols = block_cols(my_line)
    later = [None] * Y
    later[Y - 1] = jnp.zeros((PR, LANES), F32)
    for k in reversed(range(Y - 1)):
        later[k] = ys[k + 1] + later[k + 1] * (DECAY**4 * keep(my_cols, y_cols[k + 2], y_cols[k + 1]))
    zs[z] = ys[0] + later[0] * (DECAY**4 * keep(my_cols, y_cols[1], y_cols[0]))
    zs_copies = [copy(zs.at[z], zs.at[z], zs_sem, n, at(z_=k)) for n, k in enumerate(zz)]
    for n, k in enumerate(zz):
        pl.when(k < z)(zs_copies[n].start)
    reach = [
        DECAY ** (4 * (Y - 1 - k)) * keep(my_cols, chip_end, y_cols[k + 1]) for k in range(Y)
    ]
    arrive(qy_copies)
    whole = [jnp.zeros((PR, LANES), F32) for _ in range(2)]
    for k in range(Y):
        for n in range(2):
            tiles[n] = tiles[n] + folded(later[k] * qy[k, n])
            whole[n] = whole[n] + reach[k] * qy[k, n]
    for n, p in enumerate(far_first(Z)):
        pl.when(lax.rem(z + Z - p, Z) > z)(zs_copies[n].wait_recv)
    acc = jnp.zeros((PR, LANES), F32)
    for k in reversed(range(1, Z)):
        new = zs[k] + acc * (DECAY ** (4 * Y) * keep(my_cols, z_cols[k + 1], z_cols[k]))
        acc = jnp.where(k > z, new, acc)
    for n in range(2):
        wz[z, x, n : n + 1] = jnp.sum(tiles[n] + folded(acc * whole[n]), axis=0, keepdims=True)
    cross = sorted(
        ((p, q) for p in range(Z) for q in range(X) if p or q),
        key=lambda t: -min(t[0], Z - t[0]) - min(t[1], X - t[1]),
    )
    wz_copies = start([
        copy(wz.at[z, x], wz.at[z, x], wz_sem, n, at(z_=lax.rem(z + p, Z), x_=lax.rem(x + q, X)))
        for n, (p, q) in enumerate(cross)
    ])
    waiting += wz_copies
    for k in range(Y):
        ret[k, 0:PR] = (later[k] + acc * reach[k]).astype(BF16)
    r_copies = start([
        copy(ret.at[k], cr.at[core, y], r_sem, n, at(y_=k)) for n, k in enumerate(yy)
    ])
    waiting += r_copies
    cr[core, y] = ret[y]

    arrive(wz_copies)
    sums = jnp.zeros((2, LANES), F32)
    for k in range(Z):
        for q in range(X):
            sums = sums + wz[k, q]
    wy[my_line] = sums
    wy_copies = start([
        copy(wy.at[my_line], wy.at[my_line], wy_sem, n, dev) for n, dev in enumerate(lines)
    ])
    waiting += wy_copies
    arrive(r_copies)
    cr_copies = start([copy(cr.at[core], cr.at[core], cr_sem, 0, at(c_=other))])
    waiting += cr_copies
    arrive(rest_copies)
    arrive(cr_copies)
    for m_ in range(PIECES):
        r, c = rows_cols(m_)
        chip = cr[m_ % 2, m_ // 2].astype(F32)[0:PR]
        within = cx[m_ % 2, m_ // 2] + chip * (
            DECAY**2 * keep(block_cols(m_), chip_col2, chip_col1)
        )
        carry[r, c] = jnp.where(first, within, chip)

    prior_b = carry[...] * keep_12
    stores = []
    for f in (1, 0):
        moved = pltpu.roll(prior_b, lax.rem(WINDOW - (row0, row1)[f], WINDOW), 0)[0:BLOCK]
        prior = pltpu.roll(moved, (PUPIL - (col0, col1)[f]) & (PUPIL - 1), 1)
        out[f] = grad[f, 0:BLOCK] + prior
        stores.append(pltpu.make_async_copy(out.at[f], out_h.at[f], out_sem.at[f]))
        stores[-1].start()
        if f == 1:
            prior_b = (gb[1] + prior_b) * keep_01

    arrive(wy_copies)
    total = wy[0]
    for k in range(1, 2 * Y):
        total = total + wy[k]
    scale = -1.0 / (PUPIL * 2.0 * 2 * Y * Z)
    wind[0] = jnp.sum(total[0:1]) * scale
    wind[1] = jnp.sum(total[1:2]) * scale
    for n, k in enumerate(zz):
        pl.when(k < z)(zs_copies[n].wait_send)
    for store in stores:
        store.wait()
    for c in waiting:
        c.wait_send()


def on_device(Y, Z, X, phases, focal, shifts, mask):
    BLOCK = PUPIL // X
    WINDOW = BLOCK + HALO
    PIECES = 2 * Y
    PR = WINDOW * 4 // PIECES
    PR16 = -(-PR // 16) * 16
    by_pupil, by_focal = transform_tables()
    smem = pl.BlockSpec(memory_space=pltpu.SMEM)
    hbm = pl.BlockSpec(memory_space=pltpu.HBM)
    V = pltpu.VMEM

    def sems(n):
        return pltpu.SemaphoreType.DMA((2, n))

    scratch = [
        V((2, BLOCK, PUPIL), BF16),
        pltpu.SMEM((2, 2), jnp.int32),
        V((BLOCK, PUPIL), jnp.int32),
        V((PUPIL + HALO, PUPIL), BF16),
        V((PUPIL, PUPIL), BF16),
        V((4, BLOCK, 256), BF16),
        V((PUPIL, 256), BF16),
        V((2, FOCAL, LANES), BF16),
        V((HALO, PUPIL), BF16),
        V((HALO, PUPIL), BF16),
        V((2, PUPIL), F32),
        V((2, PUPIL), F32),
        V((Y, 2, 2, LANES), jnp.int32),
        V((Z, 2, LANES), jnp.int32),
        V((PUPIL, 256), BF16),
        V((X, WINDOW, 256), BF16),
        V((X, WINDOW, 256), BF16),
        V((2, WINDOW, PUPIL), F32),
        V((2, WINDOW, PUPIL), F32),
        V((2, Y, PR, LANES), F32),
        V((2, Y, PR, LANES), F32),
        V((Y, PR, LANES), F32),
        V((Y, PR, LANES), F32),
        V((Z, PR, LANES), F32),
        V((Y, PR16, LANES), BF16),
        V((2, Y, PR16, LANES), BF16),
        V((WINDOW, PUPIL), F32),
        V((2, WINDOW, PUPIL), F32),
        V((2, WINDOW, PUPIL), F32),
        V((2, Y, 2, PR, LANES), F32),
        V((Y, 2, PR, LANES), F32),
        V((Y, 2, PR, LANES), F32),
        V((Y, 2, PR, LANES), F32),
        V((Z, X, 2, LANES), F32),
        V((2 * Y, 2, LANES), F32),
        V((2, BLOCK, PUPIL), F32),
        pltpu.SemaphoreType.DMA((6,)),
        pltpu.SemaphoreType.DMA((2,)),
        sems(X), sems(X), sems(2), sems(2 * Y), sems(Z), sems(X), sems(2), sems(Y), sems(Z), sems(Y),
        sems(1), sems(1), sems(Y), sems(X * Z), sems(2 * Y), sems(1), pltpu.SemaphoreType.REGULAR,
    ]
    shapes = (
        jax.ShapeDtypeStruct((2, BLOCK, PUPIL), F32),
        jax.ShapeDtypeStruct((2,), F32),
    )
    return pl.pallas_call(
        functools.partial(body, Y, Z, X),
        name="adjoint_sweep",
        out_shape=shapes,
        in_specs=[hbm] * 6,
        out_specs=(hbm, smem),
        scratch_shapes=scratch,
        compiler_params=pltpu.CompilerParams(
            collective_id=1, has_side_effects=True, vmem_limit_bytes=63 << 20
        ),
    )(phases, focal, shifts, mask, jnp.asarray(by_pupil), jnp.asarray(by_focal))


def solution(mesh):
    X = mesh.shape["rows"]
    count = mesh.shape["tm"]
    Y = 8 if count == 128 else 2
    Z = count // (2 * Y)
    in_specs = (P("tm", "rows", None), P("tm", None, "rows", None), P("tm", None), P("rows", None))
    out_specs = (P("tm", "rows", None), P())
    return jax.shard_map(
        functools.partial(on_device, Y, Z, X), mesh=mesh, in_specs=in_specs, out_specs=out_specs,
        check_vma=False,
    )
```
